32 devices in a mesh: row: 4 (over y, core), col: 8 (over z, x).
Axes of the slice: x: 2, y: 2, z: 4, core: 2. Of those that a mesh axis runs over, the one named last changes fastest.
Arguments:
- trailing: bfloat16 [4096, 4096], P('row', 'col'), may hold values from -6 to 6
- left_outer: bfloat16 [384, 4096], P('col', 'row'), may hold values from -0.625 to 0.625
- left_inner: bfloat16 [384, 4096], P('col', 'row'), may hold values from -0.1875 to 0.1875
- upper_outer: bfloat16 [384, 4096], P('row', 'col'), may hold values from -6 to 6
- upper_inner: bfloat16 [384, 4096], P('row', 'col'), may hold values from -0.3125 to 0.3125
- left_ranks: int32 [4, 4], replicated, may hold values from 16 to 96
- upper_ranks: int32 [4, 4], replicated, may hold values from 16 to 96
Outputs:
- updated: bfloat16 [4096, 4096], P('row', 'col')
- next_panel: bfloat16 [4096, 1024], P(('row', 'col'))
The draws below stay inside these ranges and needn't reach their ends.
All inputs are finite; a program needn't handle non-finite values.
Results may differ from the reference program's by a relative error of at most 0.0042.
Values may be sent and summed in bfloat16 or wider, within the bound.
A program may use at most 64 MiB of HBM per device.

```python
import jax
import jax.numpy as jnp
from jax import lax

B = 1024
R = 96
NT = 4
ORDER = 4096
N_ROW = 4


def set_ends(drawn, rng, smallest, high):
    longest = drawn.shape.index(max(drawn.shape))
    spots = []
    for shift in (0, 1):
        where = [jax.random.randint(jax.random.fold_in(rng, axis), (), 0, length) for axis, length in enumerate(drawn.shape)]
        where[longest] = (where[longest] + shift) % drawn.shape[longest]
        spots.append(tuple(where))
    return drawn.at[spots[0]].set(smallest).at[spots[1]].set(high)


def levels(stream_key, extent, cuts, smallest, high):
    loudness, own = 1.0, jax.random.fold_in(stream_key, 6)
    for dim, shards_of in cuts:
        steps = jnp.exp(jax.random.uniform(jax.random.fold_in(own, dim), (shards_of,), jnp.float32, smallest / len(cuts), high / len(cuts)))
        loudness = loudness * jnp.repeat(steps, extent[dim] // shards_of).reshape([-1 if axis == dim else 1 for axis in range(len(extent))])
    return loudness


def noise(rng, shape, scale, reach, split=(), kind=jnp.bfloat16):
    result = scale * jax.random.normal(rng, shape, jnp.float32)
    if split:
        result = result * levels(rng, shape, split, -0.22, 0.18)
    return jnp.clip(result, -reach, reach).astype(kind)


def setup_inputs(seed: int = 0) -> dict:
    seeds = jax.random.split(jax.random.key(seed), 8)
    trailing = noise(seeds[0], (ORDER, ORDER), 1.0, 6.0, ((0, 4), (1, 8)))
    left_outer = noise(seeds[1], (NT * R, ORDER), R ** -0.5, 0.625, ((0, 8), (1, 4)))
    left_inner = noise(seeds[2], (NT * R, ORDER), B ** -0.5, 0.1875, ((0, 8), (1, 4)))
    upper_outer = noise(seeds[3], (NT * R, ORDER), 1.0, 6.0, ((0, 4), (1, 8)))
    upper_inner = noise(seeds[4], (NT * R, ORDER), (NT * R) ** -0.5, 0.3125, ((0, 4), (1, 8)))
    left_ranks = set_ends(jax.random.randint(seeds[5], (NT, NT), R // 6, R + 1), jax.random.fold_in(seeds[5], 1), R // 6, R).astype(jnp.int32)
    upper_ranks = set_ends(jax.random.randint(seeds[6], (NT, NT), R // 6, R + 1), jax.random.fold_in(seeds[6], 1), R // 6, R).astype(jnp.int32)
    return dict(trailing=trailing, left_outer=left_outer, left_inner=left_inner, upper_outer=upper_outer, upper_inner=upper_inner, left_ranks=left_ranks, upper_ranks=upper_ranks)


def reference(trailing, left_outer, left_inner, upper_outer, upper_inner, left_ranks, upper_ranks):
    tile_count = N_ROW
    rank_index = jnp.arange(R, dtype=jnp.int32)

    def tile_row(row_tile):
        outer_rows = lax.dynamic_slice_in_dim(left_outer, row_tile * B, B, 1).reshape(tile_count, R, B).astype(jnp.float32)
        interior_rows = lax.dynamic_slice_in_dim(left_inner, row_tile * B, B, 1).reshape(tile_count, R, B).astype(jnp.float32)
        row_ranks = lax.dynamic_index_in_dim(left_ranks, row_tile, 0, keepdims=False)
        left_live = (rank_index[None, :] < row_ranks[:, None]).astype(jnp.float32)

        def tile_col(col_tile):
            top_rows = lax.dynamic_slice_in_dim(upper_outer, col_tile * B, B, 1).reshape(tile_count, R, B).astype(jnp.float32)
            upper_cols = lax.dynamic_slice_in_dim(upper_inner, col_tile * B, B, 1)
            col_ranks = lax.dynamic_index_in_dim(upper_ranks, col_tile, 1, keepdims=False)
            upper_live = (rank_index[None, :] < col_ranks[:, None]).astype(jnp.float32)
            central_block = jnp.einsum("rao,rho->rah", interior_rows, top_rows)
            central_block = (central_block * left_live[:, :, None] * upper_live[:, None, :]).astype(jnp.bfloat16)
            outer_sum = jnp.einsum("ktp,ktu->pku", outer_rows, central_block.astype(jnp.float32))
            outer_sum = outer_sum.reshape(B, tile_count * R).astype(jnp.bfloat16)
            product = jnp.dot(outer_sum, upper_cols, preferred_element_type=jnp.float32)
            dense_block = lax.dynamic_slice(trailing, (row_tile * B, col_tile * B), (B, B)).astype(jnp.float32)
            return (dense_block - product).astype(jnp.bfloat16)

        row_tiles = lax.map(tile_col, jnp.arange(tile_count, dtype=jnp.int32))
        return jnp.transpose(row_tiles, (1, 0, 2)).reshape(B, tile_count * B)

    updated = lax.map(tile_row, jnp.arange(tile_count, dtype=jnp.int32)).reshape(tile_count * B, tile_count * B)
    next_panel = updated[:, 0:B]
    return (updated, next_panel)
```

```python
import functools

import jax
import jax.numpy as jnp
from jax import lax
from jax.experimental import pallas as pl
from jax.experimental.pallas import tpu as pltpu
from jax.sharding import PartitionSpec as P

MESH = pl.DeviceIdType.MESH
LANES = 128
F32 = jnp.float32
BF16 = jnp.bfloat16


def sem_names(n, nh):
    names = ["px", "x0", "q1", "p1", "z1", "zx", "zc", "cx", "c0", "c0x", "pfx"]
    for s in range(1, n):
        names += [f"xb{s}", f"xa{s}", f"yb{s}", f"ya{s}", f"cb{s}", f"ca{s}"]
        names += [f"fw{s}", f"ow{s}"]
    for d in range(1, nh):
        names += [f"p{a}{d}" for a in "ghijkl"]
    return {name: at for at, name in enumerate(names)}


def kernel(n, names, tr_in, x_in, y_in, p_in, q_in, lr, ur, up_out, np_out,
           xg, yg, pg, qg, q0g, cb, c0, og, og0, prod0, tr, ub, pf, pin, nb,
           ssem, rsem, lsem):
    nh = n // 2
    rank = p_in.shape[0]
    hr = x_in.shape[0]
    tile, width = tr_in.shape
    sr = np_out.shape[0]
    row, col = lax.axis_index("row"), lax.axis_index("col")
    zz, h = col // 2, col % 2
    oh = 1 - h
    hi, core = row // 2, row % 2
    mate = hi * 2 + (1 - core)
    xn = (row, zz * 2 + oh)
    up = (row, lax.rem(zz + 1, n) * 2 + h)
    down = (row, lax.rem(zz + n - 1, n) * 2 + h)
    first, rest = zz == 0, zz > 0
    has_up, has_down = zz < n - 1, zz > 0
    pending = []

    def on(cond, f):
        if cond is None:
            f()
        else:
            pl.when(cond)(f)

    def desc(name, src, dst, dev):
        at = names[name]
        return pltpu.make_async_remote_copy(
            src_ref=src(), dst_ref=dst(), send_sem=ssem.at[at], recv_sem=rsem.at[at],
            device_id=dev, device_id_type=MESH)

    def go(name, src, dst, dev, cond=None, sem=None):
        def make():
            at = names[sem or name]
            return pltpu.make_async_remote_copy(
                src_ref=src(), dst_ref=dst(), send_sem=ssem.at[names[name]],
                recv_sem=rsem.at[at], device_id=dev, device_id_type=MESH)
        on(cond, lambda: make().start())
        pending.append((cond, lambda: make().wait_send()))

    def got(name, dst, cond=None):
        on(cond, lambda: desc(name, dst, dst, xn).wait_recv())

    def local(at, src, dst, cond=None):
        def make():
            return pltpu.make_async_copy(src(), dst(), lsem.at[at])
        on(cond, lambda: make().start())
        return lambda: on(cond, lambda: make().wait())

    partners = [xn, (mate, col)]
    for s in range(1, n):
        partners.append((row, lax.rem(zz + s, n) * 2 + h))
    for d in range(1, nh):
        partners.append((lax.rem(hi + d, nh) * 2 + core, col))
    barrier = pltpu.get_barrier_semaphore()
    for dev in partners:
        pl.semaphore_signal(barrier, inc=1, device_id=dev, device_id_type=MESH)
    pl.semaphore_wait(barrier, len(partners))

    def ref(r):
        return lambda: r

    pd = pl.ds(0, rank)
    for nm, src, dst in (("y", y_in, lambda k: yg.at[k]), ("x", x_in, lambda k: xg.at[k, h])):
        go(nm + "b1", ref(src), lambda dst=dst: dst(zz), up, has_up)
        go(nm + "a1", ref(src), lambda dst=dst: dst(zz), down, has_down)
    go("px", ref(p_in), lambda: pg.at[row, h, pd], xn)
    go("x0", ref(x_in), lambda: xg.at[zz, h], xn)
    go("z1", ref(q_in), lambda: q0g.at[row, h, pd], up, first)
    go("zx", ref(q_in), lambda: q0g.at[row, h, pd], xn, first)
    go("q1", ref(q_in), lambda: qg.at[row, pd], (mate, col))
    for d in range(1, nh):
        go(f"pg{d}", ref(q_in), lambda: qg.at[row, pd], (lax.rem(hi + d, nh) * 2 + core, col))
    w_p = local(0, ref(p_in), lambda: pg.at[row, h, pd])
    w_x = local(1, ref(x_in), lambda: xg.at[zz, h])
    w_y = local(2, ref(y_in), lambda: yg.at[zz])
    w_q = local(3, ref(q_in), lambda: qg.at[row, pd])
    w_q0 = local(4, ref(q_in), lambda: q0g.at[row, h, pd], first)

    def rows_of(z, side):
        return pl.ds(pl.multiple_of((z * 2 + side) * sr, sr), sr)

    go("pfx", lambda: tr_in.at[rows_of(0, oh)], lambda: pin.at[h], xn, first)
    for s in range(n - 1, 0, -1):
        go(f"fw{s}", lambda s=s: tr_in.at[rows_of(s, oh)], ref(pf), (row, s * 2 + h), first, "fw1")
    for s in range(n - 1, 0, -1):
        go(f"ow{s}", lambda s=s: tr_in.at[rows_of(s, h)], lambda: pin.at[h], (row, s * 2 + h), first, "ow1")
    w_pin = local(5, lambda: tr_in.at[rows_of(0, h)], lambda: pin.at[h], first)
    w_tr = local(6, ref(tr_in), ref(tr))

    pad = LANES - rank
    pg[:, :, rank:, :] = jnp.zeros((n, 2, pad, width), BF16)
    qg[:, rank:, :] = jnp.zeros((n, pad, width), BF16)
    q0g[:, :, rank:, :] = jnp.zeros((n, 2, pad, width), BF16)

    w_p()
    got("px", lambda: pg.at[row, oh, pd])
    go("p1", lambda: pg.at[row, :, pd], lambda: pg.at[row, :, pd], (mate, col))
    for d in range(1, nh):
        go(f"ph{d}", lambda: pg.at[row, :, pd], lambda: pg.at[row, :, pd],
           (lax.rem(hi + d, nh) * 2 + core, col))

    def relay(s):
        for side, dev, ok, more, slot in (
            ("b", up, zz - s >= 0, (zz - s >= 0) & has_up, lax.rem(zz - s + n, n)),
            ("a", down, zz + s < n, (zz + s < n) & has_down, lax.rem(zz + s, n)),
        ):
            for nm, dst in (("y", lambda slot=slot: yg.at[slot]), ("x", lambda slot=slot: xg.at[slot, h])):
                got(f"{nm}{side}{s}", dst, ok)
                if s + 1 < n:
                    go(f"{nm}{side}{s + 1}", dst, dst, dev, more)
                if nm == "x":
                    go(f"c{side}{s}", dst, dst, xn, ok)

    relay(1)
    got("z1", lambda: q0g.at[row, h, pd], rest)
    mine = lambda: q0g.at[row, h, pd]
    go("z1", mine, mine, up, rest & has_up)
    go("zx", mine, mine, xn, rest)
    w_q0()
    got("zx", lambda: q0g.at[row, oh, pd])
    go("zc", lambda: q0g.at[row, :, pd], lambda: q0g.at[row, :, pd], (mate, col))
    for d in range(1, nh):
        go(f"pi{d}", lambda: q0g.at[row, :, pd], lambda: q0g.at[row, :, pd],
           (lax.rem(hi + d, nh) * 2 + core, col))

    def far(d):
        return lax.rem(hi + nh - d, nh) * 2 + core

    def far_mate(d):
        return lax.rem(hi + nh - d, nh) * 2 + 1 - core

    def second(first_name, second_name, view):
        for d in range(1, nh):
            got(f"{first_name}{d}", lambda d=d: view(far(d)))
            go(f"{second_name}{d}", lambda d=d: view(far(d)), lambda d=d: view(far(d)), (mate, col))

    def all_in(near_name, second_name, view):
        got(near_name, lambda: view(mate))
        for d in range(1, nh):
            got(f"{second_name}{d}", lambda d=d: view(far_mate(d)))

    pv = lambda k: pg.at[k, :, pd]
    qv = lambda k: qg.at[k, pd]
    zv = lambda k: q0g.at[k, :, pd]
    second("ph", "pj", pv)
    second("pg", "pk", qv)
    for s in range(2, n):
        relay(s)
    second("pi", "pl", zv)
    all_in("p1", "pj", pv)
    w_y()

    t_at = lax.broadcasted_iota(jnp.int32, (hr, LANES), 0) + h * hr
    u_at = lax.broadcasted_iota(jnp.int32, (hr, LANES), 1)
    nt = (((1,), (1,)), ((), ()))
    tn = (((0,), (0,)), ((), ()))
    for k in range(n):
        value = sum(
            lax.dot_general(yg[k, :, i * width:(i + 1) * width], pg[k, i], nt, preferred_element_type=F32)
            for i in range(2)
        )
        live = (t_at < lr[row, k]) & (u_at < ur[k, zz])
        cb[k, pl.ds(h, 1)] = jnp.where(live, value, 0.0).astype(BF16)[None]
    go("cx", lambda: cb.at[:, h], lambda: cb.at[:, h], xn)
    got("cx", lambda: cb.at[:, oh])

    def keep():
        c0[...] = cb[...]
    on(first, keep)
    half = lambda: c0.at[:, h]
    go("c0", half, half, up, first)

    all_in("q1", "pk", qv)
    w_q()
    w_x()
    got("x0", lambda: xg.at[zz, oh])
    for s in range(1, n):
        got(f"cb{s}", lambda s=s: xg.at[lax.rem(zz - s + n, n), oh], zz - s >= 0)
        got(f"ca{s}", lambda s=s: xg.at[lax.rem(zz + s, n), oh], zz + s < n)
    w_tr()
    step = 256

    def update(at, _):
        rows = pl.ds(pl.multiple_of(at * step, step), step)
        for k in range(n):
            part = xg[k, :, :, rows].reshape(2 * hr, step)
            og[:, k * LANES:(k + 1) * LANES] = lax.dot_general(
                part, cb[k].reshape(2 * hr, LANES), tn, preferred_element_type=F32).astype(BF16)
        product = jnp.dot(og[...], qg[...].reshape(n * LANES, width), preferred_element_type=F32)
        ub[rows, :] = (tr[rows, :].astype(F32) - product).astype(BF16)
        return 0

    lax.fori_loop(0, tile // step, update, 0)
    w_up = local(7, ref(ub), ref(up_out))

    got("fw1", ref(pf), rest)
    go("pfx", ref(pf), lambda: pin.at[h], xn, rest)
    got("c0", half, rest)
    go("c0", half, half, up, rest & has_up)
    go("c0x", half, half, xn, rest)
    got("c0x", lambda: c0.at[:, oh], rest)
    all_in("zc", "pl", zv)
    blk = og0.shape[0]
    lanes = pl.ds(pl.multiple_of(col * sr // blk * blk, blk), blk)
    inside = pl.ds(pl.multiple_of(lax.rem(col * sr, blk), sr), sr)
    for k in range(n):
        part = xg[k, :, :, lanes].reshape(2 * hr, blk)
        og0[:, k * LANES:(k + 1) * LANES] = lax.dot_general(
            part, c0[k].reshape(2 * hr, LANES), tn, preferred_element_type=F32).astype(BF16)
    for i in range(2):
        prod0[i] = jnp.dot(og0[...], q0g[:, i].reshape(n * LANES, width), preferred_element_type=F32)
    got("pfx", lambda: pin.at[oh])
    w_pin()
    got("ow1", lambda: pin.at[h], rest)
    for i in range(2):
        nb[:, i * width:(i + 1) * width] = (pin[i].astype(F32) - prod0[i, inside, :]).astype(BF16)
    w_np = local(8, ref(nb), ref(np_out))
    for cond, f in pending:
        on(cond, f)
    w_up()
    w_np()


def body(trailing, left_outer, left_inner, upper_outer, upper_inner, left_ranks, upper_ranks):
    n = lax.axis_size("row")
    nc = lax.axis_size("col")
    tile, width = trailing.shape
    hr = left_outer.shape[0]
    sr = tile // nc
    blk = max(sr, LANES)
    names = sem_names(n, n // 2)
    any_space = pl.BlockSpec(memory_space=pl.ANY)
    smem = pl.BlockSpec(memory_space=pltpu.SMEM)
    vmem = pltpu.VMEM
    return pl.pallas_call(
        functools.partial(kernel, n, names),
        out_shape=(
            jax.ShapeDtypeStruct((tile, width), BF16),
            jax.ShapeDtypeStruct((sr, 2 * width), BF16),
        ),
        in_specs=[any_space] * 5 + [smem] * 2,
        out_specs=(any_space, any_space),
        scratch_shapes=[
            vmem((n, 2, hr, tile), BF16),
            vmem((n, hr, tile), BF16),
            vmem((n, 2, LANES, width), BF16),
            vmem((n, LANES, width), BF16),
            vmem((n, 2, LANES, width), BF16),
            vmem((n, 2, hr, LANES), BF16),
            vmem((n, 2, hr, LANES), BF16),
            vmem((256, n * LANES), BF16),
            vmem((blk, n * LANES), BF16),
            vmem((2, blk, width), F32),
            vmem((tile, width), BF16),
            vmem((tile, width), BF16),
            vmem((sr, width), BF16),
            vmem((2, sr, width), BF16),
            vmem((sr, 2 * width), BF16),
            pltpu.SemaphoreType.DMA((len(names),)),
            pltpu.SemaphoreType.DMA((len(names),)),
            pltpu.SemaphoreType.DMA((9,)),
        ],
        compiler_params=pltpu.CompilerParams(
            collective_id=0, has_side_effects=True, vmem_limit_bytes=44 * 2 ** 20
        ),
        cost_estimate=pl.CostEstimate(
            flops=2 * tile * width * n * LANES, bytes_accessed=4 * tile * width, transcendentals=0
        ),
    )(trailing, left_outer, left_inner, upper_outer, upper_inner, left_ranks, upper_ranks)


def solution(mesh):
    in_specs = (
        P("row", "col"),
        P("col", "row"),
        P("col", "row"),
        P("row", "col"),
        P("row", "col"),
        P(),
        P(),
    )
    out_specs = (P("row", "col"), P(("row", "col"), None))
    return jax.shard_map(body, mesh=mesh, in_specs=in_specs, out_specs=out_specs, check_vma=False)
```

```python
import functools

import jax
import jax.numpy as jnp
from jax import lax
from jax.experimental import pallas as pl
from jax.experimental.pallas import tpu as pltpu
from jax.sharding import PartitionSpec as P

MESH = pl.DeviceIdType.MESH
LANES = 128
F32 = jnp.float32
BF16 = jnp.bfloat16


def sem_names(n, nh):
    names = ["px", "x0", "q1", "p1", "z1", "zx", "zc", "cx", "c0", "c0x", "pfx"]
    for s in range(1, n):
        names += [f"xb{s}", f"xa{s}", f"yb{s}", f"ya{s}", f"cb{s}", f"ca{s}"]
        names += [f"fw{s}", f"ow{s}"]
    for d in range(1, nh):
        names += [f"p{a}{d}" for a in "ghijkl"]
    return {name: at for at, name in enumerate(names)}


def kernel(n, names, tr_in, x_in, y_in, p_in, q_in, lr, ur, up_out, np_out,
           xg, yg, pg, qg, q0g, cb, c0, og, og0, prod0, tr, ub, pf, pin, nb,
           ssem, rsem, lsem):
    nh = n // 2
    rank = p_in.shape[0]
    hr = x_in.shape[0]
    tile, width = tr_in.shape
    sr = np_out.shape[0]
    row, col = lax.axis_index("row"), lax.axis_index("col")
    zz, h = col // 2, col % 2
    oh = 1 - h
    hi, core = row // 2, row % 2
    mate = hi * 2 + (1 - core)
    xn = (row, zz * 2 + oh)
    up = (row, lax.rem(zz + 1, n) * 2 + h)
    down = (row, lax.rem(zz + n - 1, n) * 2 + h)
    first, rest = zz == 0, zz > 0
    has_up, has_down = zz < n - 1, zz > 0
    pending = []

    def on(cond, f):
        if cond is None:
            f()
        else:
            pl.when(cond)(f)

    def desc(name, src, dst, dev):
        at = names[name]
        return pltpu.make_async_remote_copy(
            src_ref=src(), dst_ref=dst(), send_sem=ssem.at[at], recv_sem=rsem.at[at],
            device_id=dev, device_id_type=MESH)

    def go(name, src, dst, dev, cond=None, sem=None):
        def make():
            at = names[sem or name]
            return pltpu.make_async_remote_copy(
                src_ref=src(), dst_ref=dst(), send_sem=ssem.at[names[name]],
                recv_sem=rsem.at[at], device_id=dev, device_id_type=MESH)
        on(cond, lambda: make().start())
        pending.append((cond, lambda: make().wait_send()))

    def got(name, dst, cond=None):
        on(cond, lambda: desc(name, dst, dst, xn).wait_recv())

    def local(at, src, dst, cond=None):
        def make():
            return pltpu.make_async_copy(src(), dst(), lsem.at[at])
        on(cond, lambda: make().start())
        return lambda: on(cond, lambda: make().wait())

    partners = [xn, (mate, col)]
    for s in range(1, n):
        partners.append((row, lax.rem(zz + s, n) * 2 + h))
    for d in range(1, nh):
        partners.append((lax.rem(hi + d, nh) * 2 + core, col))
    barrier = pltpu.get_barrier_semaphore()
    for dev in partners:
        pl.semaphore_signal(barrier, inc=1, device_id=dev, device_id_type=MESH)
    pl.semaphore_wait(barrier, len(partners))

    def ref(r):
        return lambda: r

    pd = pl.ds(0, rank)
    for nm, src, dst in (("y", y_in, lambda k: yg.at[k]), ("x", x_in, lambda k: xg.at[k, h])):
        go(nm + "b1", ref(src), lambda dst=dst: dst(zz), up, has_up)
        go(nm + "a1", ref(src), lambda dst=dst: dst(zz), down, has_down)
    go("px", ref(p_in), lambda: pg.at[row, h, pd], xn)
    go("x0", ref(x_in), lambda: xg.at[zz, h], xn)
    go("z1", ref(q_in), lambda: q0g.at[row, h, pd], up, first)
    go("zx", ref(q_in), lambda: q0g.at[row, h, pd], xn, first)
    go("q1", ref(q_in), lambda: qg.at[row, pd], (mate, col))
    for d in range(1, nh):
        go(f"pg{d}", ref(q_in), lambda: qg.at[row, pd], (lax.rem(hi + d, nh) * 2 + core, col))
    w_p = local(0, ref(p_in), lambda: pg.at[row, h, pd])
    w_x = local(1, ref(x_in), lambda: xg.at[zz, h])
    w_y = local(2, ref(y_in), lambda: yg.at[zz])
    w_q = local(3, ref(q_in), lambda: qg.at[row, pd])
    w_q0 = local(4, ref(q_in), lambda: q0g.at[row, h, pd], first)

    def rows_of(z, side):
        return pl.ds(pl.multiple_of((z * 2 + side) * sr, sr), sr)

    go("pfx", lambda: tr_in.at[rows_of(0, oh)], lambda: pin.at[h], xn, first)

    def feed(s):
        go(f"fw{s}", lambda: tr_in.at[rows_of(s, oh)], ref(pf), (row, s * 2 + h), first, "fw1")
        go(f"ow{s}", lambda: tr_in.at[rows_of(s, h)], lambda: pin.at[h], (row, s * 2 + h), first, "ow1")

    w_pin = local(5, lambda: tr_in.at[rows_of(0, h)], lambda: pin.at[h], first)
    w_tr = local(6, ref(tr_in), ref(tr))

    pad = LANES - rank
    pg[:, :, rank:, :] = jnp.zeros((n, 2, pad, width), BF16)
    qg[:, rank:, :] = jnp.zeros((n, pad, width), BF16)
    q0g[:, :, rank:, :] = jnp.zeros((n, 2, pad, width), BF16)

    w_p()
    got("px", lambda: pg.at[row, oh, pd])
    go("p1", lambda: pg.at[row, :, pd], lambda: pg.at[row, :, pd], (mate, col))
    for d in range(1, nh):
        go(f"ph{d}", lambda: pg.at[row, :, pd], lambda: pg.at[row, :, pd],
           (lax.rem(hi + d, nh) * 2 + core, col))

    def relay(s):
        for side, dev, ok, more, slot in (
            ("b", up, zz - s >= 0, (zz - s >= 0) & has_up, lax.rem(zz - s + n, n)),
            ("a", down, zz + s < n, (zz + s < n) & has_down, lax.rem(zz + s, n)),
        ):
            for nm, dst in (("y", lambda slot=slot: yg.at[slot]), ("x", lambda slot=slot: xg.at[slot, h])):
                got(f"{nm}{side}{s}", dst, ok)
                if s + 1 < n:
                    go(f"{nm}{side}{s + 1}", dst, dst, dev, more)
                if nm == "x":
                    go(f"c{side}{s}", dst, dst, xn, ok)

    relay(1)
    feed(1)
    got("z1", lambda: q0g.at[row, h, pd], rest)
    mine = lambda: q0g.at[row, h, pd]
    go("z1", mine, mine, up, rest & has_up)
    go("zx", mine, mine, xn, rest)
    w_q0()
    got("zx", lambda: q0g.at[row, oh, pd])
    go("zc", lambda: q0g.at[row, :, pd], lambda: q0g.at[row, :, pd], (mate, col))
    for d in range(1, nh):
        go(f"pi{d}", lambda: q0g.at[row, :, pd], lambda: q0g.at[row, :, pd],
           (lax.rem(hi + d, nh) * 2 + core, col))

    def far(d):
        return lax.rem(hi + nh - d, nh) * 2 + core

    def far_mate(d):
        return lax.rem(hi + nh - d, nh) * 2 + 1 - core

    def second(first_name, second_name, view):
        for d in range(1, nh):
            got(f"{first_name}{d}", lambda d=d: view(far(d)))
            go(f"{second_name}{d}", lambda d=d: view(far(d)), lambda d=d: view(far(d)), (mate, col))

    def all_in(near_name, second_name, view):
        got(near_name, lambda: view(mate))
        for d in range(1, nh):
            got(f"{second_name}{d}", lambda d=d: view(far_mate(d)))

    pv = lambda k: pg.at[k, :, pd]
    qv = lambda k: qg.at[k, pd]
    zv = lambda k: q0g.at[k, :, pd]
    second("ph", "pj", pv)
    second("pg", "pk", qv)
    for s in range(2, n):
        relay(s)
        feed(s)
    second("pi", "pl", zv)
    all_in("p1", "pj", pv)
    w_y()

    t_at = lax.broadcasted_iota(jnp.int32, (hr, LANES), 0) + h * hr
    u_at = lax.broadcasted_iota(jnp.int32, (hr, LANES), 1)
    nt = (((1,), (1,)), ((), ()))
    tn = (((0,), (0,)), ((), ()))
    for k in range(n):
        value = sum(
            lax.dot_general(yg[k, :, i * width:(i + 1) * width], pg[k, i], nt, preferred_element_type=F32)
            for i in range(2)
        )
        live = (t_at < lr[row, k]) & (u_at < ur[k, zz])
        cb[k, pl.ds(h, 1)] = jnp.where(live, value, 0.0).astype(BF16)[None]
    go("cx", lambda: cb.at[:, h], lambda: cb.at[:, h], xn)
    got("cx", lambda: cb.at[:, oh])

    def keep():
        c0[...] = cb[...]
    on(first, keep)
    half = lambda: c0.at[:, h]
    go("c0", half, half, up, first)

    all_in("q1", "pk", qv)
    w_q()
    w_x()
    got("x0", lambda: xg.at[zz, oh])
    for s in range(1, n):
        got(f"cb{s}", lambda s=s: xg.at[lax.rem(zz - s + n, n), oh], zz - s >= 0)
        got(f"ca{s}", lambda s=s: xg.at[lax.rem(zz + s, n), oh], zz + s < n)
    w_tr()
    step = 256

    def update(at, _):
        rows = pl.ds(pl.multiple_of(at * step, step), step)
        for k in range(n):
            part = xg[k, :, :, rows].reshape(2 * hr, step)
            og[:, k * LANES:(k + 1) * LANES] = lax.dot_general(
                part, cb[k].reshape(2 * hr, LANES), tn, preferred_element_type=F32).astype(BF16)
        product = jnp.dot(og[...], qg[...].reshape(n * LANES, width), preferred_element_type=F32)
        ub[rows, :] = (tr[rows, :].astype(F32) - product).astype(BF16)
        return 0

    lax.fori_loop(0, tile // step, update, 0)
    w_up = local(7, ref(ub), ref(up_out))

    got("fw1", ref(pf), rest)
    go("pfx", ref(pf), lambda: pin.at[h], xn, rest)
    got("c0", half, rest)
    go("c0", half, half, up, rest & has_up)
    go("c0x", half, half, xn, rest)
    got("c0x", lambda: c0.at[:, oh], rest)
    all_in("zc", "pl", zv)
    blk = og0.shape[0]
    lanes = pl.ds(pl.multiple_of(col * sr // blk * blk, blk), blk)
    inside = pl.ds(pl.multiple_of(lax.rem(col * sr, blk), sr), sr)
    for k in range(n):
        part = xg[k, :, :, lanes].reshape(2 * hr, blk)
        og0[:, k * LANES:(k + 1) * LANES] = lax.dot_general(
            part, c0[k].reshape(2 * hr, LANES), tn, preferred_element_type=F32).astype(BF16)
    for i in range(2):
        prod0[i] = jnp.dot(og0[...], q0g[:, i].reshape(n * LANES, width), preferred_element_type=F32)
    got("pfx", lambda: pin.at[oh])
    w_pin()
    got("ow1", lambda: pin.at[h], rest)
    for i in range(2):
        nb[:, i * width:(i + 1) * width] = (pin[i].astype(F32) - prod0[i, inside, :]).astype(BF16)
    w_np = local(8, ref(nb), ref(np_out))
    for cond, f in pending:
        on(cond, f)
    w_up()
    w_np()


def body(trailing, left_outer, left_inner, upper_outer, upper_inner, left_ranks, upper_ranks):
    n = lax.axis_size("row")
    nc = lax.axis_size("col")
    tile, width = trailing.shape
    hr = left_outer.shape[0]
    sr = tile // nc
    blk = max(sr, LANES)
    names = sem_names(n, n // 2)
    any_space = pl.BlockSpec(memory_space=pl.ANY)
    smem = pl.BlockSpec(memory_space=pltpu.SMEM)
    vmem = pltpu.VMEM
    return pl.pallas_call(
        functools.partial(kernel, n, names),
        out_shape=(
            jax.ShapeDtypeStruct((tile, width), BF16),
            jax.ShapeDtypeStruct((sr, 2 * width), BF16),
        ),
        in_specs=[any_space] * 5 + [smem] * 2,
        out_specs=(any_space, any_space),
        scratch_shapes=[
            vmem((n, 2, hr, tile), BF16),
            vmem((n, hr, tile), BF16),
            vmem((n, 2, LANES, width), BF16),
            vmem((n, LANES, width), BF16),
            vmem((n, 2, LANES, width), BF16),
            vmem((n, 2, hr, LANES), BF16),
            vmem((n, 2, hr, LANES), BF16),
            vmem((256, n * LANES), BF16),
            vmem((blk, n * LANES), BF16),
            vmem((2, blk, width), F32),
            vmem((tile, width), BF16),
            vmem((tile, width), BF16),
            vmem((sr, width), BF16),
            vmem((2, sr, width), BF16),
            vmem((sr, 2 * width), BF16),
            pltpu.SemaphoreType.DMA((len(names),)),
            pltpu.SemaphoreType.DMA((len(names),)),
            pltpu.SemaphoreType.DMA((9,)),
        ],
        compiler_params=pltpu.CompilerParams(
            collective_id=0, has_side_effects=True, vmem_limit_bytes=60 * 2 ** 20
        ),
        cost_estimate=pl.CostEstimate(
            flops=2 * tile * width * n * LANES, bytes_accessed=4 * tile * width, transcendentals=0
        ),
    )(trailing, left_outer, left_inner, upper_outer, upper_inner, left_ranks, upper_ranks)


def solution(mesh):
    in_specs = (
        P("row", "col"),
        P("col", "row"),
        P("col", "row"),
        P("row", "col"),
        P("row", "col"),
        P(),
        P(),
    )
    out_specs = (P("row", "col"), P(("row", "col"), None))
    return jax.shard_map(body, mesh=mesh, in_specs=in_specs, out_specs=out_specs, check_vma=False)
```

```python
import functools

import jax
import jax.numpy as jnp
from jax import lax
from jax.experimental import pallas as pl
from jax.experimental.pallas import tpu as pltpu
from jax.sharding import PartitionSpec as P

MESH = pl.DeviceIdType.MESH
LANES = 128
F32 = jnp.float32
BF16 = jnp.bfloat16


def sem_names(n, nh):
    names = ["px", "x0", "q1", "p1", "z1", "zx", "zc", "cx", "c0", "c0x", "pfx"]
    for s in range(1, n):
        names += [f"xb{s}", f"xa{s}", f"yb{s}", f"ya{s}", f"cb{s}", f"ca{s}"]
        names += [f"fw{s}", f"ow{s}"]
    for d in range(1, nh):
        names += [f"p{a}{d}" for a in "ghijkl"]
    return {name: at for at, name in enumerate(names)}


def kernel(n, names, tr_in, x_in, y_in, p_in, q_in, lr, ur, up_out, np_out,
           xg, yg, pg, qg, q0g, cb, c0, og, og0, prod0, tr, ub, pf, pin, nb,
           ssem, rsem, lsem):
    nh = n // 2
    rank = p_in.shape[0]
    hr = x_in.shape[0]
    tile, width = tr_in.shape
    sr = np_out.shape[0]
    row, col = lax.axis_index("row"), lax.axis_index("col")
    zz, h = col // 2, col % 2
    oh = 1 - h
    hi, core = row // 2, row % 2
    mate = hi * 2 + (1 - core)
    xn = (row, zz * 2 + oh)
    up = (row, lax.rem(zz + 1, n) * 2 + h)
    down = (row, lax.rem(zz + n - 1, n) * 2 + h)
    first, rest = zz == 0, zz > 0
    has_up, has_down = zz < n - 1, zz > 0
    pending = []

    def on(cond, f):
        if cond is None:
            f()
        else:
            pl.when(cond)(f)

    def desc(name, src, dst, dev):
        at = names[name]
        return pltpu.make_async_remote_copy(
            src_ref=src(), dst_ref=dst(), send_sem=ssem.at[at], recv_sem=rsem.at[at],
            device_id=dev, device_id_type=MESH)

    def go(name, src, dst, dev, cond=None, sem=None):
        def make():
            at = names[sem or name]
            return pltpu.make_async_remote_copy(
                src_ref=src(), dst_ref=dst(), send_sem=ssem.at[names[name]],
                recv_sem=rsem.at[at], device_id=dev, device_id_type=MESH)
        on(cond, lambda: make().start())
        pending.append((name, cond, lambda: make().wait_send()))

    def sent(name):
        for entry in [e for e in pending if e[0] == name]:
            on(*entry[1:])
            pending.remove(entry)

    def got(name, dst, cond=None):
        on(cond, lambda: desc(name, dst, dst, xn).wait_recv())

    def local(at, src, dst, cond=None):
        def make():
            return pltpu.make_async_copy(src(), dst(), lsem.at[at])
        on(cond, lambda: make().start())
        return lambda: on(cond, lambda: make().wait())

    partners = [xn, (mate, col)]
    for s in range(1, n):
        partners.append((row, lax.rem(zz + s, n) * 2 + h))
    for d in range(1, nh):
        partners.append((lax.rem(hi + d, nh) * 2 + core, col))
    barrier = pltpu.get_barrier_semaphore()
    for dev in partners:
        pl.semaphore_signal(barrier, inc=1, device_id=dev, device_id_type=MESH)
    pl.semaphore_wait(barrier, len(partners))

    def ref(r):
        return lambda: r

    pd = pl.ds(0, rank)
    for nm, src, dst in (("y", y_in, lambda k: yg.at[k]), ("x", x_in, lambda k: xg.at[k, h])):
        go(nm + "b1", ref(src), lambda dst=dst: dst(zz), up, has_up)
        go(nm + "a1", ref(src), lambda dst=dst: dst(zz), down, has_down)
    go("px", ref(p_in), lambda: pg.at[row, h, pd], xn)
    go("q1", ref(q_in), lambda: qg.at[row, pd], (mate, col))
    for d in range(1, nh):
        go(f"pg{d}", ref(q_in), lambda: qg.at[row, pd], (lax.rem(hi + d, nh) * 2 + core, col))
    w_p = local(0, ref(p_in), lambda: pg.at[row, h, pd])
    w_x = local(1, ref(x_in), lambda: xg.at[zz, h])
    w_y = local(2, ref(y_in), lambda: yg.at[zz])
    w_q = local(3, ref(q_in), lambda: qg.at[row, pd])
    w_q0 = local(4, ref(q_in), lambda: q0g.at[row, h, pd], first)

    def rows_of(z, side):
        return pl.ds(pl.multiple_of((z * 2 + side) * sr, sr), sr)

    go("pfx", lambda: tr_in.at[rows_of(0, oh)], lambda: pin.at[h], xn, first)

    def across(s):
        go(f"fw{s}", lambda: tr_in.at[rows_of(s, oh)], ref(pf), (row, s * 2 + h), first, "fw1")

    def along(s):
        go(f"ow{s}", lambda: tr_in.at[rows_of(s, h)], lambda: pin.at[h], (row, s * 2 + h), first, "ow1")

    w_pin = local(5, lambda: tr_in.at[rows_of(0, h)], lambda: pin.at[h], first)
    w_tr = local(6, ref(tr_in), ref(tr))

    pad = LANES - rank
    pg[:, :, rank:, :] = jnp.zeros((n, 2, pad, width), BF16)
    qg[:, rank:, :] = jnp.zeros((n, pad, width), BF16)
    q0g[:, :, rank:, :] = jnp.zeros((n, 2, pad, width), BF16)

    w_p()
    got("px", lambda: pg.at[row, oh, pd])
    go("x0", ref(x_in), lambda: xg.at[zz, h], xn)
    go("zx", ref(q_in), lambda: q0g.at[row, h, pd], xn, first)
    go("p1", lambda: pg.at[row, :, pd], lambda: pg.at[row, :, pd], (mate, col))
    for d in range(1, nh):
        go(f"ph{d}", lambda: pg.at[row, :, pd], lambda: pg.at[row, :, pd],
           (lax.rem(hi + d, nh) * 2 + core, col))

    def relay(s):
        for side, dev, ok, more, slot in (
            ("b", up, zz - s >= 0, (zz - s >= 0) & has_up, lax.rem(zz - s + n, n)),
            ("a", down, zz + s < n, (zz + s < n) & has_down, lax.rem(zz + s, n)),
        ):
            for nm, dst in (("y", lambda slot=slot: yg.at[slot]), ("x", lambda slot=slot: xg.at[slot, h])):
                got(f"{nm}{side}{s}", dst, ok)
                if s + 1 < n:
                    go(f"{nm}{side}{s + 1}", dst, dst, dev, more)
                if nm == "x":
                    go(f"c{side}{s}", dst, dst, xn, ok)

    def far(d):
        return lax.rem(hi + nh - d, nh) * 2 + core

    def far_mate(d):
        return lax.rem(hi + nh - d, nh) * 2 + 1 - core

    def second(first_name, second_name, view):
        for d in range(1, nh):
            got(f"{first_name}{d}", lambda d=d: view(far(d)))
            go(f"{second_name}{d}", lambda d=d: view(far(d)), lambda d=d: view(far(d)), (mate, col))

    def all_in(near_name, second_name, view):
        got(near_name, lambda: view(mate))
        for d in range(1, nh):
            got(f"{second_name}{d}", lambda d=d: view(far_mate(d)))

    pv = lambda k: pg.at[k, :, pd]
    qv = lambda k: qg.at[k, pd]
    zv = lambda k: q0g.at[k, :, pd]
    mine = lambda: q0g.at[row, h, pd]
    relay(1)
    go("z1", ref(q_in), mine, up, first)
    across(1)
    second("pg", "pk", qv)
    for s in range(2, n):
        relay(s)
        if s == 2:
            second("ph", "pj", pv)
        if s < n - 1:
            along(s - 1)
        across(s)

    def first_column(cond, more):
        got("z1", mine, cond)
        if more:
            go("z1", mine, mine, up, cond)
        go("zx", mine, mine, xn, cond)

    middle, last = rest & has_up, zz == n - 1
    first_column(middle, True)
    all_in("p1", "pj", pv)
    w_y()

    t_at = lax.broadcasted_iota(jnp.int32, (hr, LANES), 0) + h * hr
    u_at = lax.broadcasted_iota(jnp.int32, (hr, LANES), 1)
    nt = (((1,), (1,)), ((), ()))
    tn = (((0,), (0,)), ((), ()))
    for k in range(n):
        value = sum(
            lax.dot_general(yg[k, :, i * width:(i + 1) * width], pg[k, i], nt, preferred_element_type=F32)
            for i in range(2)
        )
        live = (t_at < lr[row, k]) & (u_at < ur[k, zz])
        cb[k, pl.ds(h, 1)] = jnp.where(live, value, 0.0).astype(BF16)[None]
    go("cx", lambda: cb.at[:, h], lambda: cb.at[:, h], xn)
    first_column(last, False)
    sent("fw1")
    sent(f"fw{n - 2}")
    along(n - 2)
    got("cx", lambda: cb.at[:, oh])

    def keep():
        c0[...] = cb[...]
    on(first, keep)
    half = lambda: c0.at[:, h]
    go("c0", half, half, up, first)
    w_q0()
    got("zx", lambda: q0g.at[row, oh, pd])
    go("zc", lambda: q0g.at[row, :, pd], lambda: q0g.at[row, :, pd], (mate, col))
    for d in range(1, nh):
        go(f"pi{d}", lambda: q0g.at[row, :, pd], lambda: q0g.at[row, :, pd],
           (lax.rem(hi + d, nh) * 2 + core, col))

    def relay_first(cond, more):
        got("fw1", ref(pf), cond)
        go("pfx", ref(pf), lambda: pin.at[h], xn, cond)
        got("c0", half, cond)
        if more:
            go("c0", half, half, up, cond)
        go("c0x", half, half, xn, cond)

    relay_first(middle, True)

    all_in("q1", "pk", qv)
    w_q()
    w_x()
    got("x0", lambda: xg.at[zz, oh])
    for s in range(1, n):
        got(f"cb{s}", lambda s=s: xg.at[lax.rem(zz - s + n, n), oh], zz - s >= 0)
        got(f"ca{s}", lambda s=s: xg.at[lax.rem(zz + s, n), oh], zz + s < n)
    w_tr()
    step = 256

    def update(at, _):
        rows = pl.ds(pl.multiple_of(at * step, step), step)
        for k in range(n):
            part = xg[k, :, :, rows].reshape(2 * hr, step)
            og[:, k * LANES:(k + 1) * LANES] = lax.dot_general(
                part, cb[k].reshape(2 * hr, LANES), tn, preferred_element_type=F32).astype(BF16)
        product = jnp.dot(og[...], qg[...].reshape(n * LANES, width), preferred_element_type=F32)
        ub[rows, :] = (tr[rows, :].astype(F32) - product).astype(BF16)
        return 0

    lax.fori_loop(0, tile // step, update, 0)
    w_up = local(7, ref(ub), ref(up_out))

    sent(f"fw{n - 1}")
    along(n - 1)
    second("pi", "pl", zv)
    relay_first(last, False)
    got("c0x", lambda: c0.at[:, oh], rest)
    all_in("zc", "pl", zv)
    blk = og0.shape[0]
    lanes = pl.ds(pl.multiple_of(col * sr // blk * blk, blk), blk)
    inside = pl.ds(pl.multiple_of(lax.rem(col * sr, blk), sr), sr)
    for k in range(n):
        part = xg[k, :, :, lanes].reshape(2 * hr, blk)
        og0[:, k * LANES:(k + 1) * LANES] = lax.dot_general(
            part, c0[k].reshape(2 * hr, LANES), tn, preferred_element_type=F32).astype(BF16)
    for i in range(2):
        prod0[i] = jnp.dot(og0[...], q0g[:, i].reshape(n * LANES, width), preferred_element_type=F32)
    got("pfx", lambda: pin.at[oh])
    w_pin()
    got("ow1", lambda: pin.at[h], rest)
    for i in range(2):
        nb[:, i * width:(i + 1) * width] = (pin[i].astype(F32) - prod0[i, inside, :]).astype(BF16)
    w_np = local(8, ref(nb), ref(np_out))
    for entry in pending:
        on(*entry[1:])
    w_up()
    w_np()


def body(trailing, left_outer, left_inner, upper_outer, upper_inner, left_ranks, upper_ranks):
    n = lax.axis_size("row")
    nc = lax.axis_size("col")
    tile, width = trailing.shape
    hr = left_outer.shape[0]
    sr = tile // nc
    blk = max(sr, LANES)
    names = sem_names(n, n // 2)
    any_space = pl.BlockSpec(memory_space=pl.ANY)
    smem = pl.BlockSpec(memory_space=pltpu.SMEM)
    vmem = pltpu.VMEM
    return pl.pallas_call(
        functools.partial(kernel, n, names),
        out_shape=(
            jax.ShapeDtypeStruct((tile, width), BF16),
            jax.ShapeDtypeStruct((sr, 2 * width), BF16),
        ),
        in_specs=[any_space] * 5 + [smem] * 2,
        out_specs=(any_space, any_space),
        scratch_shapes=[
            vmem((n, 2, hr, tile), BF16),
            vmem((n, hr, tile), BF16),
            vmem((n, 2, LANES, width), BF16),
            vmem((n, LANES, width), BF16),
            vmem((n, 2, LANES, width), BF16),
            vmem((n, 2, hr, LANES), BF16),
            vmem((n, 2, hr, LANES), BF16),
            vmem((256, n * LANES), BF16),
            vmem((blk, n * LANES), BF16),
            vmem((2, blk, width), F32),
            vmem((tile, width), BF16),
            vmem((tile, width), BF16),
            vmem((sr, width), BF16),
            vmem((2, sr, width), BF16),
            vmem((sr, 2 * width), BF16),
            pltpu.SemaphoreType.DMA((len(names),)),
            pltpu.SemaphoreType.DMA((len(names),)),
            pltpu.SemaphoreType.DMA((9,)),
        ],
        compiler_params=pltpu.CompilerParams(
            collective_id=0, has_side_effects=True, vmem_limit_bytes=56 * 2 ** 20
        ),
        cost_estimate=pl.CostEstimate(
            flops=2 * tile * width * n * LANES, bytes_accessed=4 * tile * width, transcendentals=0
        ),
    )(trailing, left_outer, left_inner, upper_outer, upper_inner, left_ranks, upper_ranks)


def solution(mesh):
    in_specs = (
        P("row", "col"),
        P("col", "row"),
        P("col", "row"),
        P("row", "col"),
        P("row", "col"),
        P(),
        P(),
    )
    out_specs = (P("row", "col"), P(("row", "col"), None))
    return jax.shard_map(body, mesh=mesh, in_specs=in_specs, out_specs=out_specs, check_vma=False)
```

```python
import functools

import jax
import jax.numpy as jnp
from jax import lax
from jax.experimental import pallas as pl
from jax.experimental.pallas import tpu as pltpu
from jax.sharding import PartitionSpec as P

MESH = pl.DeviceIdType.MESH
LANES = 128
F32 = jnp.float32
BF16 = jnp.bfloat16


def sem_names(n, nh):
    names = ["px", "x0", "q1", "p1", "q1p", "z1", "zc", "cx", "c0", "c0x", "pfx"]
    for s in range(1, n):
        names += [f"xb{s}", f"xa{s}", f"yb{s}", f"ya{s}", f"cb{s}", f"ca{s}"]
        names += [f"fw{s}", f"ow{s}"]
    for d in range(1, nh):
        names += [f"p{a}{d}" for a in "ghijklmn"]
    return {name: at for at, name in enumerate(names)}


def kernel(n, names, tr_in, x_in, y_in, p_in, q_in, lr, ur, up_out, np_out,
           xg, yg, pg, qg, q0g, cb, c0, og, og0, prod0, tr, ub, raw, nb,
           ssem, rsem, lsem):
    nh = n // 2
    rank = p_in.shape[0]
    hr = x_in.shape[0]
    tile, width = tr_in.shape
    sr = np_out.shape[0]
    row, col = lax.axis_index("row"), lax.axis_index("col")
    zz, h = col // 2, col % 2
    oh = 1 - h
    hi, core = row // 2, row % 2
    mate = hi * 2 + (1 - core)
    xn = (row, zz * 2 + oh)
    up = (row, lax.rem(zz + 1, n) * 2 + h)
    down = (row, lax.rem(zz + n - 1, n) * 2 + h)
    first, rest = zz == 0, zz > 0
    has_up, has_down = zz < n - 1, zz > 0
    pending = []

    def on(cond, f):
        if cond is None:
            f()
        else:
            pl.when(cond)(f)

    def desc(name, src, dst, dev):
        at = names[name]
        return pltpu.make_async_remote_copy(
            src_ref=src(), dst_ref=dst(), send_sem=ssem.at[at], recv_sem=rsem.at[at],
            device_id=dev, device_id_type=MESH)

    def go(name, src, dst, dev, cond=None, sem=None):
        def make():
            at = names[sem or name]
            return pltpu.make_async_remote_copy(
                src_ref=src(), dst_ref=dst(), send_sem=ssem.at[names[name]],
                recv_sem=rsem.at[at], device_id=dev, device_id_type=MESH)
        on(cond, lambda: make().start())
        pending.append((name, cond, lambda: make().wait_send()))

    def sent(name):
        for entry in [e for e in pending if e[0] == name]:
            on(*entry[1:])
            pending.remove(entry)

    def got(name, dst, cond=None):
        on(cond, lambda: desc(name, dst, dst, xn).wait_recv())

    def local(at, src, dst, cond=None):
        def make():
            return pltpu.make_async_copy(src(), dst(), lsem.at[at])
        on(cond, lambda: make().start())
        return lambda: on(cond, lambda: make().wait())

    partners = [xn, (mate, col)]
    for s in range(1, n):
        partners.append((row, lax.rem(zz + s, n) * 2 + h))
    for d in range(1, nh):
        partners.append((lax.rem(hi + d, nh) * 2 + core, col))
    barrier = pltpu.get_barrier_semaphore()
    for dev in partners:
        pl.semaphore_signal(barrier, inc=1, device_id=dev, device_id_type=MESH)
    pl.semaphore_wait(barrier, len(partners))

    def ref(r):
        return lambda: r

    pd = pl.ds(0, rank)
    fars = [(d, (lax.rem(hi + d, nh) * 2 + core, col)) for d in range(1, nh)]
    near = (mate, col)
    middle, last = rest & has_up, zz == n - 1
    yv, xv = (lambda k: yg.at[k]), (lambda k: xg.at[k, h])
    pv = lambda side: lambda k: pg.at[k, side, pd]
    qv, zv = (lambda k: qg.at[k, pd]), (lambda k: q0g.at[k, pd])

    def spread(near_name, far_name, view, src=None):
        src = src or (lambda: view(row))
        go(near_name, src, lambda: view(row), near)
        for d, dev in fars:
            go(f"{far_name}{d}", src, lambda: view(row), dev)

    def far(d):
        return lax.rem(hi + nh - d, nh) * 2 + core

    def far_mate(d):
        return lax.rem(hi + nh - d, nh) * 2 + 1 - core

    def second(first_name, second_name, view, cond=None):
        for d in range(1, nh):
            got(f"{first_name}{d}", lambda d=d: view(far(d)), cond)
            go(f"{second_name}{d}", lambda d=d: view(far(d)), lambda d=d: view(far(d)), near, cond)

    def all_in(near_name, second_name, view, cond=None):
        got(near_name, lambda: view(mate), cond)
        for d in range(1, nh):
            got(f"{second_name}{d}", lambda d=d: view(far_mate(d)), cond)

    go("yb1", ref(y_in), lambda: yv(zz), up, has_up)
    go("ya1", ref(y_in), lambda: yv(zz), down, has_down)
    go("px", ref(p_in), lambda: pv(h)(row), xn)
    spread("p1", "pg", pv(h), ref(p_in))
    w_p = local(0, ref(p_in), lambda: pv(h)(row))
    w_x = local(1, ref(x_in), lambda: xv(zz))
    w_y = local(2, ref(y_in), lambda: yv(zz))
    w_q = local(3, ref(q_in), lambda: qv(row))

    def rows_of(z, side):
        return pl.ds(pl.multiple_of((z * 2 + side) * sr, sr), sr)

    def across(s):
        go(f"fw{s}", lambda: tr_in.at[rows_of(s, oh)], lambda: raw.at[oh], (row, s * 2 + h), first, "fw1")

    def along(s):
        go(f"ow{s}", lambda: tr_in.at[rows_of(s, h)], lambda: raw.at[h], (row, s * 2 + h), first, "ow1")

    w_raw = [local(5 + i, lambda i=i: tr_in.at[rows_of(0, i)], lambda i=i: raw.at[i], first) for i in range(2)]
    w_tr = local(7, ref(tr_in), ref(tr))

    pad = LANES - rank
    pg[:, :, rank:, :] = jnp.zeros((n, 2, pad, width), BF16)
    qg[:, rank:, :] = jnp.zeros((n, pad, width), BF16)

    def pad_first():
        q0g[:, rank:, :] = jnp.zeros((n, pad, width), BF16)
    on(rest, pad_first)

    got("px", lambda: pv(oh)(row))
    spread("q1p", "ph", pv(oh))

    def relay(nm, s, view):
        for side, dev, ok, more, slot in (
            ("b", up, zz - s >= 0, (zz - s >= 0) & has_up, lax.rem(zz - s + n, n)),
            ("a", down, zz + s < n, (zz + s < n) & has_down, lax.rem(zz + s, n)),
        ):
            dst = lambda slot=slot: view(slot)
            got(f"{nm}{side}{s}", dst, ok)
            if s + 1 < n:
                go(f"{nm}{side}{s + 1}", dst, dst, dev, more)
            if nm == "x":
                go(f"c{side}{s}", dst, dst, xn, ok)

    relay("y", 1, yv)
    go("xb1", ref(x_in), lambda: xv(zz), up, first)
    across(1)
    second("pg", "pi", pv(h))
    for s in range(2, n):
        relay("y", s, yv)
        if s == 2:
            go("xb1", ref(x_in), lambda: xv(zz), up, middle)
            go("xa1", ref(x_in), lambda: xv(zz), down, has_down)
            go("x0", ref(x_in), lambda: xv(zz), xn)
            go("z1", ref(q_in), lambda: zv(row), up, first)
            along(1)
            second("ph", "pj", pv(oh))
    spread("q1", "pk", qv, ref(q_in))
    w_p()
    w_y()
    all_in("p1", "pi", pv(h))
    all_in("q1p", "pj", pv(oh))

    t_at = lax.broadcasted_iota(jnp.int32, (hr, LANES), 0) + h * hr
    u_at = lax.broadcasted_iota(jnp.int32, (hr, LANES), 1)
    nt = (((1,), (1,)), ((), ()))
    tn = (((0,), (0,)), ((), ()))
    for k in range(n):
        value = sum(
            lax.dot_general(yg[k, :, i * width:(i + 1) * width], pg[k, i], nt, preferred_element_type=F32)
            for i in range(2)
        )
        live = (t_at < lr[row, k]) & (u_at < ur[k, zz])
        cb[k, pl.ds(h, 1)] = jnp.where(live, value, 0.0).astype(BF16)[None]
    go("cx", lambda: cb.at[:, h], lambda: cb.at[:, h], xn)
    relay("x", 1, xv)
    got("cx", lambda: cb.at[:, oh])

    def keep():
        c0[...] = cb[...]
    on(first, keep)
    half = lambda: c0.at[:, h]
    go("c0", half, half, up, first)
    if n > 2:
        across(2)

    def first_column(cond, more):
        got("z1", lambda: zv(row), cond)
        if more:
            go("z1", lambda: zv(row), lambda: zv(row), up, cond)
        go("zc", lambda: zv(row), lambda: zv(row), near, cond)
        for d, dev in fars:
            go(f"pl{d}", lambda: zv(row), lambda: zv(row), dev, cond)

    def relay_core(cond, more):
        got("c0", half, cond)
        if more:
            go("c0", half, half, up, cond)
        go("c0x", half, half, xn, cond)

    first_column(middle, True)
    relay("x", 2, xv)
    relay_core(middle, True)
    for s in range(3, n):
        relay("x", s, xv)
        across(s)
    first_column(last, False)
    second("pk", "pm", qv)
    for s in range(2, n - 1):
        sent(f"fw{s}")
        along(s)
    relay_core(last, False)

    all_in("q1", "pm", qv)
    w_q()
    w_x()
    got("x0", lambda: xg.at[zz, oh])
    for s in range(1, n):
        got(f"cb{s}", lambda s=s: xg.at[lax.rem(zz - s + n, n), oh], zz - s >= 0)
        got(f"ca{s}", lambda s=s: xg.at[lax.rem(zz + s, n), oh], zz + s < n)
    w_tr()
    step = 256

    def update(at, _):
        rows = pl.ds(pl.multiple_of(at * step, step), step)
        for k in range(n):
            part = xg[k, :, :, rows].reshape(2 * hr, step)
            og[:, k * LANES:(k + 1) * LANES] = lax.dot_general(
                part, cb[k].reshape(2 * hr, LANES), tn, preferred_element_type=F32).astype(BF16)
        product = jnp.dot(og[...], qg[...].reshape(n * LANES, width), preferred_element_type=F32)
        ub[rows, :] = (tr[rows, :].astype(F32) - product).astype(BF16)
        return 0

    lax.fori_loop(0, tile // step, update, 0)
    w_up = local(4, ref(ub), ref(up_out))
    sent(f"fw{n - 1}")
    along(n - 1)

    second("pl", "pn", zv, rest)
    got("c0x", lambda: c0.at[:, oh], rest)
    all_in("zc", "pn", zv, rest)

    def same():
        q0g[...] = qg[...]
    on(first, same)
    blk = og0.shape[0]
    start = zz * 2 * sr
    lanes = pl.ds(pl.multiple_of(start // blk * blk, blk), blk)
    for k in range(n):
        part = xg[k, :, :, lanes].reshape(2 * hr, blk)
        og0[:, k * LANES:(k + 1) * LANES] = lax.dot_general(
            part, c0[k].reshape(2 * hr, LANES), tn, preferred_element_type=F32).astype(BF16)
    prod0[...] = jnp.dot(og0[...], q0g[...].reshape(n * LANES, width), preferred_element_type=F32)

    def finish(side, at):
        inside = pl.ds(pl.multiple_of(lax.rem(start, blk) + side * sr, sr), sr)
        nb[at] = (raw[side].astype(F32) - prod0[inside, :]).astype(BF16)

    def columns(side):
        return np_out.at[:, pl.ds(pl.multiple_of(side * width, width), width)]

    for w in w_raw:
        w()
    got("fw1", lambda: raw.at[oh], rest)
    finish(oh, 0)
    go("pfx", lambda: nb.at[0], lambda: columns(h), xn)
    got("ow1", lambda: raw.at[h], rest)
    finish(h, 1)
    w_np = local(8, lambda: nb.at[1], lambda: columns(h))
    got("pfx", lambda: columns(oh))
    for entry in pending:
        on(*entry[1:])
    w_up()
    w_np()


def body(trailing, left_outer, left_inner, upper_outer, upper_inner, left_ranks, upper_ranks):
    n = lax.axis_size("row")
    nc = lax.axis_size("col")
    tile, width = trailing.shape
    hr = left_outer.shape[0]
    sr = tile // nc
    blk = max(2 * sr, LANES)
    names = sem_names(n, n // 2)
    any_space = pl.BlockSpec(memory_space=pl.ANY)
    smem = pl.BlockSpec(memory_space=pltpu.SMEM)
    vmem = pltpu.VMEM
    return pl.pallas_call(
        functools.partial(kernel, n, names),
        out_shape=(
            jax.ShapeDtypeStruct((tile, width), BF16),
            jax.ShapeDtypeStruct((sr, 2 * width), BF16),
        ),
        in_specs=[any_space] * 5 + [smem] * 2,
        out_specs=(any_space, any_space),
        scratch_shapes=[
            vmem((n, 2, hr, tile), BF16),
            vmem((n, hr, tile), BF16),
            vmem((n, 2, LANES, width), BF16),
            vmem((n, LANES, width), BF16),
            vmem((n, LANES, width), BF16),
            vmem((n, 2, hr, LANES), BF16),
            vmem((n, 2, hr, LANES), BF16),
            vmem((256, n * LANES), BF16),
            vmem((blk, n * LANES), BF16),
            vmem((blk, width), F32),
            vmem((tile, width), BF16),
            vmem((tile, width), BF16),
            vmem((2, sr, width), BF16),
            vmem((2, sr, width), BF16),
            pltpu.SemaphoreType.DMA((len(names),)),
            pltpu.SemaphoreType.DMA((len(names),)),
            pltpu.SemaphoreType.DMA((9,)),
        ],
        compiler_params=pltpu.CompilerParams(
            collective_id=0, has_side_effects=True, vmem_limit_bytes=56 * 2 ** 20
        ),
        cost_estimate=pl.CostEstimate(
            flops=2 * tile * width * n * LANES, bytes_accessed=4 * tile * width, transcendentals=0
        ),
    )(trailing, left_outer, left_inner, upper_outer, upper_inner, left_ranks, upper_ranks)


def solution(mesh):
    in_specs = (
        P("row", "col"),
        P("col", "row"),
        P("col", "row"),
        P("row", "col"),
        P("row", "col"),
        P(),
        P(),
    )
    out_specs = (P("row", "col"), P(("row", "col"), None))
    return jax.shard_map(body, mesh=mesh, in_specs=in_specs, out_specs=out_specs, check_vma=False)
```

```python
import functools

import jax
import jax.numpy as jnp
from jax import lax
from jax.experimental import pallas as pl
from jax.experimental.pallas import tpu as pltpu
from jax.sharding import PartitionSpec as P

MESH = pl.DeviceIdType.MESH
LANES = 128
F32 = jnp.float32
BF16 = jnp.bfloat16


def sem_names(n, nh):
    names = ["px", "x0", "q1", "p1", "q1p", "z1", "zc", "cx", "c0", "c0x", "pfx"]
    for s in range(1, n):
        names += [f"xb{s}", f"xa{s}", f"yb{s}", f"ya{s}", f"cb{s}", f"ca{s}"]
        names += [f"fw{s}", f"ow{s}"]
    for d in range(1, nh):
        names += [f"p{a}{d}" for a in "ghijklmn"]
    return {name: at for at, name in enumerate(names)}


def kernel(n, names, tr_in, x_in, y_in, p_in, q_in, lr, ur, up_out, np_out,
           xg, yg, pg, qg, q0g, cb, c0, og, og0, prod0, tr, ub, raw, nb,
           ssem, rsem, lsem):
    nh = n // 2
    rank = p_in.shape[0]
    hr = x_in.shape[0]
    tile, width = tr_in.shape
    sr = np_out.shape[0]
    row, col = lax.axis_index("row"), lax.axis_index("col")
    zz, h = col // 2, col % 2
    oh = 1 - h
    hi, core = row // 2, row % 2
    mate = hi * 2 + (1 - core)
    xn = (row, zz * 2 + oh)
    up = (row, lax.rem(zz + 1, n) * 2 + h)
    down = (row, lax.rem(zz + n - 1, n) * 2 + h)
    first, rest = zz == 0, zz > 0
    has_up, has_down = zz < n - 1, zz > 0
    pending = []

    def on(cond, f):
        if cond is None:
            f()
        else:
            pl.when(cond)(f)

    def desc(name, src, dst, dev):
        at = names[name]
        return pltpu.make_async_remote_copy(
            src_ref=src(), dst_ref=dst(), send_sem=ssem.at[at], recv_sem=rsem.at[at],
            device_id=dev, device_id_type=MESH)

    def go(name, src, dst, dev, cond=None, sem=None):
        def make():
            at = names[sem or name]
            return pltpu.make_async_remote_copy(
                src_ref=src(), dst_ref=dst(), send_sem=ssem.at[names[name]],
                recv_sem=rsem.at[at], device_id=dev, device_id_type=MESH)
        on(cond, lambda: make().start())
        pending.append((name, cond, lambda: make().wait_send()))

    def sent(name):
        for entry in [e for e in pending if e[0] == name]:
            on(*entry[1:])
            pending.remove(entry)

    def got(name, dst, cond=None):
        on(cond, lambda: desc(name, dst, dst, xn).wait_recv())

    def local(at, src, dst, cond=None):
        def make():
            return pltpu.make_async_copy(src(), dst(), lsem.at[at])
        on(cond, lambda: make().start())
        return lambda: on(cond, lambda: make().wait())

    partners = [xn, (mate, col)]
    for s in range(1, n):
        partners.append((row, lax.rem(zz + s, n) * 2 + h))
    for d in range(1, nh):
        partners.append((lax.rem(hi + d, nh) * 2 + core, col))
    barrier = pltpu.get_barrier_semaphore()
    for dev in partners:
        pl.semaphore_signal(barrier, inc=1, device_id=dev, device_id_type=MESH)
    pl.semaphore_wait(barrier, len(partners))

    def ref(r):
        return lambda: r

    pd = pl.ds(0, rank)
    fars = [(d, (lax.rem(hi + d, nh) * 2 + core, col)) for d in range(1, nh)]
    near = (mate, col)
    middle, last = rest & has_up, zz == n - 1
    yv, xv = (lambda k: yg.at[k]), (lambda k: xg.at[k, h])
    pv = lambda side: lambda k: pg.at[k, side, pd]
    qv, zv = (lambda k: qg.at[k, pd]), (lambda k: q0g.at[k, pd])

    def spread(near_name, far_name, view, src=None):
        src = src or (lambda: view(row))
        go(near_name, src, lambda: view(row), near)
        for d, dev in fars:
            go(f"{far_name}{d}", src, lambda: view(row), dev)

    def far(d):
        return lax.rem(hi + nh - d, nh) * 2 + core

    def far_mate(d):
        return lax.rem(hi + nh - d, nh) * 2 + 1 - core

    def second(first_name, second_name, view, cond=None):
        for d in range(1, nh):
            got(f"{first_name}{d}", lambda d=d: view(far(d)), cond)
            go(f"{second_name}{d}", lambda d=d: view(far(d)), lambda d=d: view(far(d)), near, cond)

    def all_in(near_name, second_name, view, cond=None):
        got(near_name, lambda: view(mate), cond)
        for d in range(1, nh):
            got(f"{second_name}{d}", lambda d=d: view(far_mate(d)), cond)

    go("yb1", ref(y_in), lambda: yv(zz), up, has_up)
    go("ya1", ref(y_in), lambda: yv(zz), down, has_down)
    go("xb1", ref(x_in), lambda: xv(zz), up, first)
    go("px", ref(p_in), lambda: pv(h)(row), xn)
    spread("p1", "pg", pv(h), ref(p_in))
    w_p = local(0, ref(p_in), lambda: pv(h)(row))
    w_x = local(1, ref(x_in), lambda: xv(zz))
    w_y = local(2, ref(y_in), lambda: yv(zz))
    w_q = local(3, ref(q_in), lambda: qv(row))

    def rows_of(z, side):
        return pl.ds(pl.multiple_of((z * 2 + side) * sr, sr), sr)

    def across(s):
        go(f"fw{s}", lambda: tr_in.at[rows_of(s, oh)], lambda: raw.at[oh], (row, s * 2 + h), first, "fw1")

    def along(s):
        go(f"ow{s}", lambda: tr_in.at[rows_of(s, h)], lambda: raw.at[h], (row, s * 2 + h), first, "ow1")

    w_raw = [local(5 + i, lambda i=i: tr_in.at[rows_of(0, i)], lambda i=i: raw.at[i], first) for i in range(2)]
    w_tr = local(7, ref(tr_in), ref(tr))

    pad = LANES - rank
    pg[:, :, rank:, :] = jnp.zeros((n, 2, pad, width), BF16)
    qg[:, rank:, :] = jnp.zeros((n, pad, width), BF16)

    def pad_first():
        q0g[:, rank:, :] = jnp.zeros((n, pad, width), BF16)
    on(rest, pad_first)

    got("px", lambda: pv(oh)(row))
    spread("q1p", "ph", pv(oh))

    def relay(nm, s, view):
        for side, dev, ok, more, slot in (
            ("b", up, zz - s >= 0, (zz - s >= 0) & has_up, lax.rem(zz - s + n, n)),
            ("a", down, zz + s < n, (zz + s < n) & has_down, lax.rem(zz + s, n)),
        ):
            dst = lambda slot=slot: view(slot)
            got(f"{nm}{side}{s}", dst, ok)
            if s + 1 < n:
                go(f"{nm}{side}{s + 1}", dst, dst, dev, more)
            if nm == "x":
                go(f"c{side}{s}", dst, dst, xn, ok)

    relay("y", 1, yv)
    go("xb1", ref(x_in), lambda: xv(zz), up, middle)
    go("xa1", ref(x_in), lambda: xv(zz), down, has_down)
    go("x0", ref(x_in), lambda: xv(zz), xn)
    across(1)
    second("pg", "pi", pv(h))
    for s in range(2, n):
        relay("y", s, yv)
        if s == 2:
            go("z1", ref(q_in), lambda: zv(row), up, first)
            along(1)
            relay("x", 1, xv)
            second("ph", "pj", pv(oh))
    spread("q1", "pk", qv, ref(q_in))
    w_p()
    w_y()
    all_in("p1", "pi", pv(h))
    all_in("q1p", "pj", pv(oh))

    t_at = lax.broadcasted_iota(jnp.int32, (hr, LANES), 0) + h * hr
    u_at = lax.broadcasted_iota(jnp.int32, (hr, LANES), 1)
    nt = (((1,), (1,)), ((), ()))
    tn = (((0,), (0,)), ((), ()))
    for k in range(n):
        value = sum(
            lax.dot_general(yg[k, :, i * width:(i + 1) * width], pg[k, i], nt, preferred_element_type=F32)
            for i in range(2)
        )
        live = (t_at < lr[row, k]) & (u_at < ur[k, zz])
        cb[k, pl.ds(h, 1)] = jnp.where(live, value, 0.0).astype(BF16)[None]
    go("cx", lambda: cb.at[:, h], lambda: cb.at[:, h], xn)
    relay("x", 2, xv)
    got("cx", lambda: cb.at[:, oh])

    def keep():
        c0[...] = cb[...]
    on(first, keep)
    half = lambda: c0.at[:, h]
    go("c0", half, half, up, first)
    if n > 2:
        across(2)

    def first_column(cond, more):
        got("z1", lambda: zv(row), cond)
        if more:
            go("z1", lambda: zv(row), lambda: zv(row), up, cond)
        go("zc", lambda: zv(row), lambda: zv(row), near, cond)
        for d, dev in fars:
            go(f"pl{d}", lambda: zv(row), lambda: zv(row), dev, cond)

    def relay_core(cond, more):
        got("c0", half, cond)
        if more:
            go("c0", half, half, up, cond)
        go("c0x", half, half, xn, cond)

    first_column(middle, True)
    relay_core(middle, True)
    for s in range(3, n):
        relay("x", s, xv)
        across(s)
    first_column(last, False)
    second("pk", "pm", qv)
    for s in range(2, n - 1):
        sent(f"fw{s}")
        along(s)
    relay_core(last, False)

    all_in("q1", "pm", qv)
    w_q()
    w_x()
    got("x0", lambda: xg.at[zz, oh])
    for s in range(1, n):
        got(f"cb{s}", lambda s=s: xg.at[lax.rem(zz - s + n, n), oh], zz - s >= 0)
        got(f"ca{s}", lambda s=s: xg.at[lax.rem(zz + s, n), oh], zz + s < n)
    w_tr()
    step = og.shape[0]
    for at in range(tile // step):
        rows = slice(at * step, (at + 1) * step)
        for k in range(n):
            part = xg[k, :, :, rows].reshape(2 * hr, step)
            og[:, k * LANES:(k + 1) * LANES] = lax.dot_general(
                part, cb[k].reshape(2 * hr, LANES), tn, preferred_element_type=F32).astype(BF16)
        product = jnp.dot(og[...], qg[...].reshape(n * LANES, width), preferred_element_type=F32)
        ub[rows, :] = (tr[rows, :].astype(F32) - product).astype(BF16)
        if at == 0:
            sent(f"fw{n - 1}")
            along(n - 1)
    w_up = local(4, ref(ub), ref(up_out))

    second("pl", "pn", zv, rest)
    got("c0x", lambda: c0.at[:, oh], rest)
    all_in("zc", "pn", zv, rest)

    def same():
        q0g[...] = qg[...]
    on(first, same)
    blk = og0.shape[0]
    start = zz * 2 * sr
    lanes = pl.ds(pl.multiple_of(start // blk * blk, blk), blk)
    for k in range(n):
        part = xg[k, :, :, lanes].reshape(2 * hr, blk)
        og0[:, k * LANES:(k + 1) * LANES] = lax.dot_general(
            part, c0[k].reshape(2 * hr, LANES), tn, preferred_element_type=F32).astype(BF16)
    prod0[...] = jnp.dot(og0[...], q0g[...].reshape(n * LANES, width), preferred_element_type=F32)

    def finish(side, at):
        inside = pl.ds(pl.multiple_of(lax.rem(start, blk) + side * sr, sr), sr)
        nb[at] = (raw[side].astype(F32) - prod0[inside, :]).astype(BF16)

    def columns(side):
        return np_out.at[:, pl.ds(pl.multiple_of(side * width, width), width)]

    for w in w_raw:
        w()
    got("fw1", lambda: raw.at[oh], rest)
    finish(oh, 0)
    go("pfx", lambda: nb.at[0], lambda: columns(h), xn)
    got("ow1", lambda: raw.at[h], rest)
    finish(h, 1)
    w_np = local(8, lambda: nb.at[1], lambda: columns(h))
    got("pfx", lambda: columns(oh))
    for entry in pending:
        on(*entry[1:])
    w_up()
    w_np()


def body(trailing, left_outer, left_inner, upper_outer, upper_inner, left_ranks, upper_ranks):
    n = lax.axis_size("row")
    nc = lax.axis_size("col")
    tile, width = trailing.shape
    hr = left_outer.shape[0]
    sr = tile // nc
    blk = max(2 * sr, LANES)
    names = sem_names(n, n // 2)
    any_space = pl.BlockSpec(memory_space=pl.ANY)
    smem = pl.BlockSpec(memory_space=pltpu.SMEM)
    vmem = pltpu.VMEM
    return pl.pallas_call(
        functools.partial(kernel, n, names),
        out_shape=(
            jax.ShapeDtypeStruct((tile, width), BF16),
            jax.ShapeDtypeStruct((sr, 2 * width), BF16),
        ),
        in_specs=[any_space] * 5 + [smem] * 2,
        out_specs=(any_space, any_space),
        scratch_shapes=[
            vmem((n, 2, hr, tile), BF16),
            vmem((n, hr, tile), BF16),
            vmem((n, 2, LANES, width), BF16),
            vmem((n, LANES, width), BF16),
            vmem((n, LANES, width), BF16),
            vmem((n, 2, hr, LANES), BF16),
            vmem((n, 2, hr, LANES), BF16),
            vmem((512, n * LANES), BF16),
            vmem((blk, n * LANES), BF16),
            vmem((blk, width), F32),
            vmem((tile, width), BF16),
            vmem((tile, width), BF16),
            vmem((2, sr, width), BF16),
            vmem((2, sr, width), BF16),
            pltpu.SemaphoreType.DMA((len(names),)),
            pltpu.SemaphoreType.DMA((len(names),)),
            pltpu.SemaphoreType.DMA((9,)),
        ],
        compiler_params=pltpu.CompilerParams(
            collective_id=0, has_side_effects=True, vmem_limit_bytes=56 * 2 ** 20
        ),
        cost_estimate=pl.CostEstimate(
            flops=2 * tile * width * n * LANES, bytes_accessed=4 * tile * width, transcendentals=0
        ),
    )(trailing, left_outer, left_inner, upper_outer, upper_inner, left_ranks, upper_ranks)


def solution(mesh):
    in_specs = (
        P("row", "col"),
        P("col", "row"),
        P("col", "row"),
        P("row", "col"),
        P("row", "col"),
        P(),
        P(),
    )
    out_specs = (P("row", "col"), P(("row", "col"), None))
    return jax.shard_map(body, mesh=mesh, in_specs=in_specs, out_specs=out_specs, check_vma=False)
```

```python
import functools

import jax
import jax.numpy as jnp
from jax import lax
from jax.experimental import pallas as pl
from jax.experimental.pallas import tpu as pltpu
from jax.sharding import PartitionSpec as P

MESH = pl.DeviceIdType.MESH
LANES = 128
F32 = jnp.float32
BF16 = jnp.bfloat16


def sem_names(n, nh):
    names = ["px", "x0", "q1", "p1", "q1p", "z1", "zc", "cx", "c0", "c0x", "pfx"]
    for s in range(1, n):
        names += [f"xb{s}", f"xa{s}", f"yb{s}", f"ya{s}", f"cb{s}", f"ca{s}"]
        names += [f"fw{s}", f"ow{s}"]
    for d in range(1, nh):
        names += [f"p{a}{d}" for a in "ghijklmn"]
    return {name: at for at, name in enumerate(names)}


def kernel(n, names, tr_in, x_in, y_in, p_in, q_in, lr, ur, up_out, np_out,
           xg, yg, pg, qg, q0g, cb, c0, og, og0, prod0, tr, ub, raw, nb,
           ssem, rsem, lsem):
    nh = n // 2
    rank = p_in.shape[0]
    hr = x_in.shape[0]
    tile, width = tr_in.shape
    sr = np_out.shape[0]
    row, col = lax.axis_index("row"), lax.axis_index("col")
    zz, h = col // 2, col % 2
    oh = 1 - h
    hi, core = row // 2, row % 2
    mate = hi * 2 + (1 - core)
    xn = (row, zz * 2 + oh)
    up = (row, lax.rem(zz + 1, n) * 2 + h)
    down = (row, lax.rem(zz + n - 1, n) * 2 + h)
    first, rest = zz == 0, zz > 0
    has_up, has_down = zz < n - 1, zz > 0
    pending = []

    def on(cond, f):
        if cond is None:
            f()
        else:
            pl.when(cond)(f)

    def desc(name, src, dst, dev):
        at = names[name]
        return pltpu.make_async_remote_copy(
            src_ref=src(), dst_ref=dst(), send_sem=ssem.at[at], recv_sem=rsem.at[at],
            device_id=dev, device_id_type=MESH)

    def go(name, src, dst, dev, cond=None, sem=None):
        def make():
            at = names[sem or name]
            return pltpu.make_async_remote_copy(
                src_ref=src(), dst_ref=dst(), send_sem=ssem.at[names[name]],
                recv_sem=rsem.at[at], device_id=dev, device_id_type=MESH)
        on(cond, lambda: make().start())
        pending.append((name, cond, lambda: make().wait_send()))

    def got(name, dst, cond=None):
        on(cond, lambda: desc(name, dst, dst, xn).wait_recv())

    def local(at, src, dst, cond=None):
        def make():
            return pltpu.make_async_copy(src(), dst(), lsem.at[at])
        on(cond, lambda: make().start())
        return lambda: on(cond, lambda: make().wait())

    partners = [xn, (mate, col)]
    for s in range(1, n):
        partners.append((row, lax.rem(zz + s, n) * 2 + h))
    for d in range(1, nh):
        partners.append((lax.rem(hi + d, nh) * 2 + core, col))
    barrier = pltpu.get_barrier_semaphore()
    for dev in partners:
        pl.semaphore_signal(barrier, inc=1, device_id=dev, device_id_type=MESH)
    pl.semaphore_wait(barrier, len(partners))

    def ref(r):
        return lambda: r

    pd = pl.ds(0, rank)
    fars = [(d, (lax.rem(hi + d, nh) * 2 + core, col)) for d in range(1, nh)]
    near = (mate, col)
    middle, last = rest & has_up, zz == n - 1
    yv, xv = (lambda k: yg.at[k]), (lambda k: xg.at[k, h])
    pv = lambda side: lambda k: pg.at[k, side, pd]
    qv, zv = (lambda k: qg.at[k, pd]), (lambda k: q0g.at[k, pd])

    def spread(near_name, far_name, view, src=None):
        src = src or (lambda: view(row))
        go(near_name, src, lambda: view(row), near)
        for d, dev in fars:
            go(f"{far_name}{d}", src, lambda: view(row), dev)

    def far(d):
        return lax.rem(hi + nh - d, nh) * 2 + core

    def far_mate(d):
        return lax.rem(hi + nh - d, nh) * 2 + 1 - core

    def second(first_name, second_name, view, cond=None):
        for d in range(1, nh):
            got(f"{first_name}{d}", lambda d=d: view(far(d)), cond)
            go(f"{second_name}{d}", lambda d=d: view(far(d)), lambda d=d: view(far(d)), near, cond)

    def all_in(near_name, second_name, view, cond=None):
        got(near_name, lambda: view(mate), cond)
        for d in range(1, nh):
            got(f"{second_name}{d}", lambda d=d: view(far_mate(d)), cond)

    go("yb1", ref(y_in), lambda: yv(zz), up, has_up)
    go("ya1", ref(y_in), lambda: yv(zz), down, has_down)
    go("xb1", ref(x_in), lambda: xv(zz), up, first)
    go("px", ref(p_in), lambda: pv(h)(row), xn)
    spread("p1", "pg", pv(h), ref(p_in))
    w_p = local(0, ref(p_in), lambda: pv(h)(row))
    w_x = local(1, ref(x_in), lambda: xv(zz))
    w_y = local(2, ref(y_in), lambda: yv(zz))
    w_q = local(3, ref(q_in), lambda: qv(row))

    def rows_of(z, side):
        return pl.ds(pl.multiple_of((z * 2 + side) * sr, sr), sr)

    def across(s):
        go(f"fw{s}", lambda: tr_in.at[rows_of(s, oh)], lambda: raw.at[oh], (row, s * 2 + h), first, "fw1")

    def along(s):
        go(f"ow{s}", lambda: tr_in.at[rows_of(s, h)], lambda: raw.at[h], (row, s * 2 + h), first, "ow1")

    w_raw = [local(5 + i, lambda i=i: tr_in.at[rows_of(0, i)], lambda i=i: raw.at[i], first) for i in range(2)]
    w_tr = local(7, ref(tr_in), ref(tr))

    pad = LANES - rank
    pg[:, :, rank:, :] = jnp.zeros((n, 2, pad, width), BF16)
    qg[:, rank:, :] = jnp.zeros((n, pad, width), BF16)

    def pad_first():
        q0g[:, rank:, :] = jnp.zeros((n, pad, width), BF16)
    on(rest, pad_first)

    got("px", lambda: pv(oh)(row))
    spread("q1p", "ph", pv(oh))

    def relay(nm, s, view):
        for side, dev, ok, more, slot in (
            ("b", up, zz - s >= 0, (zz - s >= 0) & has_up, lax.rem(zz - s + n, n)),
            ("a", down, zz + s < n, (zz + s < n) & has_down, lax.rem(zz + s, n)),
        ):
            dst = lambda slot=slot: view(slot)
            got(f"{nm}{side}{s}", dst, ok)
            if s + 1 < n:
                go(f"{nm}{side}{s + 1}", dst, dst, dev, more)
            if nm == "x":
                go(f"c{side}{s}", dst, dst, xn, ok)

    relay("y", 1, yv)
    go("xb1", ref(x_in), lambda: xv(zz), up, middle)
    go("xa1", ref(x_in), lambda: xv(zz), down, has_down)
    go("x0", ref(x_in), lambda: xv(zz), xn)
    go("z1", ref(q_in), lambda: zv(row), up, first)
    across(n - 1)
    second("pg", "pi", pv(h))
    def first_column(cond, more):
        got("z1", lambda: zv(row), cond)
        if more:
            go("z1", lambda: zv(row), lambda: zv(row), up, cond)
        go("zc", lambda: zv(row), lambda: zv(row), near, cond)
        for d, dev in fars:
            go(f"pl{d}", lambda: zv(row), lambda: zv(row), dev, cond)

    half = lambda: c0.at[:, h]

    def relay_core(cond, more):
        got("c0", half, cond)
        if more:
            go("c0", half, half, up, cond)
        go("c0x", half, half, xn, cond)

    for s in range(2, n):
        relay("y", s, yv)
        if s == 2:
            across(1)
            along(n - 1)
            relay("x", 1, xv)
            first_column(middle, True)
            second("ph", "pj", pv(oh))
    for s in range(n - 2, 1, -1):
        across(s)
    spread("q1", "pk", qv, ref(q_in))
    w_p()
    w_y()
    all_in("p1", "pi", pv(h))
    all_in("q1p", "pj", pv(oh))

    t_at = lax.broadcasted_iota(jnp.int32, (hr, LANES), 0) + h * hr
    u_at = lax.broadcasted_iota(jnp.int32, (hr, LANES), 1)
    nt = (((1,), (1,)), ((), ()))
    tn = (((0,), (0,)), ((), ()))
    for k in range(n):
        value = sum(
            lax.dot_general(yg[k, :, i * width:(i + 1) * width], pg[k, i], nt, preferred_element_type=F32)
            for i in range(2)
        )
        live = (t_at < lr[row, k]) & (u_at < ur[k, zz])
        cb[k, pl.ds(h, 1)] = jnp.where(live, value, 0.0).astype(BF16)[None]
    go("cx", lambda: cb.at[:, h], lambda: cb.at[:, h], xn)
    got("cx", lambda: cb.at[:, oh])

    def keep():
        c0[...] = cb[...]
    on(first, keep)
    go("c0", half, half, up, first)
    for s in range(n - 2, 1, -1):
        along(s)
    relay("x", 2, xv)
    relay_core(middle, True)
    for s in range(3, n):
        relay("x", s, xv)
    along(1)
    first_column(last, False)
    second("pk", "pm", qv)

    all_in("q1", "pm", qv)
    w_q()
    w_x()
    got("x0", lambda: xg.at[zz, oh])
    for s in range(1, n):
        got(f"cb{s}", lambda s=s: xg.at[lax.rem(zz - s + n, n), oh], zz - s >= 0)
        got(f"ca{s}", lambda s=s: xg.at[lax.rem(zz + s, n), oh], zz + s < n)
    w_tr()
    step = og.shape[0]
    for at in range(tile // step):
        rows = slice(at * step, (at + 1) * step)
        for k in range(n):
            part = xg[k, :, :, rows].reshape(2 * hr, step)
            og[:, k * LANES:(k + 1) * LANES] = lax.dot_general(
                part, cb[k].reshape(2 * hr, LANES), tn, preferred_element_type=F32).astype(BF16)
        product = jnp.dot(og[...], qg[...].reshape(n * LANES, width), preferred_element_type=F32)
        ub[rows, :] = (tr[rows, :].astype(F32) - product).astype(BF16)
    w_up = local(4, ref(ub), ref(up_out))

    relay_core(last, False)
    second("pl", "pn", zv, rest)
    got("c0x", lambda: c0.at[:, oh], rest)
    all_in("zc", "pn", zv, rest)

    def same():
        q0g[...] = qg[...]
    on(first, same)
    blk = og0.shape[0]
    start = zz * 2 * sr
    lanes = pl.ds(pl.multiple_of(start // blk * blk, blk), blk)
    for k in range(n):
        part = xg[k, :, :, lanes].reshape(2 * hr, blk)
        og0[:, k * LANES:(k + 1) * LANES] = lax.dot_general(
            part, c0[k].reshape(2 * hr, LANES), tn, preferred_element_type=F32).astype(BF16)
    prod0[...] = jnp.dot(og0[...], q0g[...].reshape(n * LANES, width), preferred_element_type=F32)

    def finish(side, at):
        inside = pl.ds(pl.multiple_of(lax.rem(start, blk) + side * sr, sr), sr)
        nb[at] = (raw[side].astype(F32) - prod0[inside, :]).astype(BF16)

    def columns(side):
        return np_out.at[:, pl.ds(pl.multiple_of(side * width, width), width)]

    for w in w_raw:
        w()
    got("fw1", lambda: raw.at[oh], rest)
    finish(oh, 0)
    go("pfx", lambda: nb.at[0], lambda: columns(h), xn)
    got("ow1", lambda: raw.at[h], rest)
    finish(h, 1)
    w_np = local(8, lambda: nb.at[1], lambda: columns(h))
    got("pfx", lambda: columns(oh))
    for entry in pending:
        on(*entry[1:])
    w_up()
    w_np()


def body(trailing, left_outer, left_inner, upper_outer, upper_inner, left_ranks, upper_ranks):
    n = lax.axis_size("row")
    nc = lax.axis_size("col")
    tile, width = trailing.shape
    hr = left_outer.shape[0]
    sr = tile // nc
    blk = max(2 * sr, LANES)
    names = sem_names(n, n // 2)
    any_space = pl.BlockSpec(memory_space=pl.ANY)
    smem = pl.BlockSpec(memory_space=pltpu.SMEM)
    vmem = pltpu.VMEM
    return pl.pallas_call(
        functools.partial(kernel, n, names),
        out_shape=(
            jax.ShapeDtypeStruct((tile, width), BF16),
            jax.ShapeDtypeStruct((sr, 2 * width), BF16),
        ),
        in_specs=[any_space] * 5 + [smem] * 2,
        out_specs=(any_space, any_space),
        scratch_shapes=[
            vmem((n, 2, hr, tile), BF16),
            vmem((n, hr, tile), BF16),
            vmem((n, 2, LANES, width), BF16),
            vmem((n, LANES, width), BF16),
            vmem((n, LANES, width), BF16),
            vmem((n, 2, hr, LANES), BF16),
            vmem((n, 2, hr, LANES), BF16),
            vmem((512, n * LANES), BF16),
            vmem((blk, n * LANES), BF16),
            vmem((blk, width), F32),
            vmem((tile, width), BF16),
            vmem((tile, width), BF16),
            vmem((2, sr, width), BF16),
            vmem((2, sr, width), BF16),
            pltpu.SemaphoreType.DMA((len(names),)),
            pltpu.SemaphoreType.DMA((len(names),)),
            pltpu.SemaphoreType.DMA((9,)),
        ],
        compiler_params=pltpu.CompilerParams(
            collective_id=0, has_side_effects=True, vmem_limit_bytes=56 * 2 ** 20
        ),
        cost_estimate=pl.CostEstimate(
            flops=2 * tile * width * n * LANES, bytes_accessed=4 * tile * width, transcendentals=0
        ),
    )(trailing, left_outer, left_inner, upper_outer, upper_inner, left_ranks, upper_ranks)


def solution(mesh):
    in_specs = (
        P("row", "col"),
        P("col", "row"),
        P("col", "row"),
        P("row", "col"),
        P("row", "col"),
        P(),
        P(),
    )
    out_specs = (P("row", "col"), P(("row", "col"), None))
    return jax.shard_map(body, mesh=mesh, in_specs=in_specs, out_specs=out_specs, check_vma=False)
```

```python
import functools

import jax
import jax.numpy as jnp
from jax import lax
from jax.experimental import pallas as pl
from jax.experimental.pallas import tpu as pltpu
from jax.sharding import PartitionSpec as P

MESH = pl.DeviceIdType.MESH
LANES = 128
F32 = jnp.float32
BF16 = jnp.bfloat16


def sem_names(n, nh):
    names = ["px", "x0", "q1", "p1", "q1p", "z1", "zc", "cx", "c0", "c0x", "pfx"]
    for s in range(1, n):
        names += [f"xb{s}", f"xa{s}", f"yb{s}", f"ya{s}", f"cb{s}", f"ca{s}"]
        names += [f"fw{s}", f"ow{s}"]
    for d in range(1, nh):
        names += [f"p{a}{d}" for a in "ghijklmn"]
    return {name: at for at, name in enumerate(names)}


def kernel(n, names, tr_in, x_in, y_in, p_in, q_in, lr, ur, up_out, np_out,
           xg, yg, pg, qg, q0g, cb, c0, og, og0, prod0, tr, ub, raw, nb,
           ssem, rsem, lsem):
    nh = n // 2
    rank = p_in.shape[0]
    hr = x_in.shape[0]
    tile, width = tr_in.shape
    sr = np_out.shape[0]
    row, col = lax.axis_index("row"), lax.axis_index("col")
    zz, h = col // 2, col % 2
    oh = 1 - h
    hi, core = row // 2, row % 2
    mate = hi * 2 + (1 - core)
    xn = (row, zz * 2 + oh)
    up = (row, lax.rem(zz + 1, n) * 2 + h)
    down = (row, lax.rem(zz + n - 1, n) * 2 + h)
    first, rest = zz == 0, zz > 0
    has_up, has_down = zz < n - 1, zz > 0
    pending = []

    def on(cond, f):
        if cond is None:
            f()
        else:
            pl.when(cond)(f)

    def desc(name, src, dst, dev):
        at = names[name]
        return pltpu.make_async_remote_copy(
            src_ref=src(), dst_ref=dst(), send_sem=ssem.at[at], recv_sem=rsem.at[at],
            device_id=dev, device_id_type=MESH)

    def go(name, src, dst, dev, cond=None, sem=None):
        def make():
            at = names[sem or name]
            return pltpu.make_async_remote_copy(
                src_ref=src(), dst_ref=dst(), send_sem=ssem.at[names[name]],
                recv_sem=rsem.at[at], device_id=dev, device_id_type=MESH)
        on(cond, lambda: make().start())
        pending.append((name, cond, lambda: make().wait_send()))

    def got(name, dst, cond=None):
        on(cond, lambda: desc(name, dst, dst, xn).wait_recv())

    def local(at, src, dst, cond=None):
        def make():
            return pltpu.make_async_copy(src(), dst(), lsem.at[at])
        on(cond, lambda: make().start())
        return lambda: on(cond, lambda: make().wait())

    partners = [xn, (mate, col)]
    for s in range(1, n):
        partners.append((row, lax.rem(zz + s, n) * 2 + h))
    for d in range(1, nh):
        partners.append((lax.rem(hi + d, nh) * 2 + core, col))
    barrier = pltpu.get_barrier_semaphore()
    for dev in partners:
        pl.semaphore_signal(barrier, inc=1, device_id=dev, device_id_type=MESH)
    pl.semaphore_wait(barrier, len(partners))

    def ref(r):
        return lambda: r

    pd = pl.ds(0, rank)
    fars = [(d, (lax.rem(hi + d, nh) * 2 + core, col)) for d in range(1, nh)]
    near = (mate, col)
    middle, last = rest & has_up, zz == n - 1
    yv, xv = (lambda k: yg.at[k]), (lambda k: xg.at[k, h])
    pv = lambda side: lambda k: pg.at[k, side, pd]
    qv, zv = (lambda k: qg.at[k, pd]), (lambda k: q0g.at[k, pd])

    def spread(near_name, far_name, view, src=None):
        src = src or (lambda: view(row))
        go(near_name, src, lambda: view(row), near)
        for d, dev in fars:
            go(f"{far_name}{d}", src, lambda: view(row), dev)

    def far(d):
        return lax.rem(hi + nh - d, nh) * 2 + core

    def far_mate(d):
        return lax.rem(hi + nh - d, nh) * 2 + 1 - core

    def second(first_name, second_name, view, cond=None):
        for d in range(1, nh):
            got(f"{first_name}{d}", lambda d=d: view(far(d)), cond)
            go(f"{second_name}{d}", lambda d=d: view(far(d)), lambda d=d: view(far(d)), near, cond)

    def all_in(near_name, second_name, view, cond=None):
        got(near_name, lambda: view(mate), cond)
        for d in range(1, nh):
            got(f"{second_name}{d}", lambda d=d: view(far_mate(d)), cond)

    go("yb1", ref(y_in), lambda: yv(zz), up, has_up)
    go("ya1", ref(y_in), lambda: yv(zz), down, has_down)
    go("xb1", ref(x_in), lambda: xv(zz), up, has_up)
    go("xa1", ref(x_in), lambda: xv(zz), down, has_down)
    go("px", ref(p_in), lambda: pv(h)(row), xn)
    spread("p1", "pg", pv(h), ref(p_in))
    w_p = local(0, ref(p_in), lambda: pv(h)(row))
    w_x = local(1, ref(x_in), lambda: xv(zz))
    w_y = local(2, ref(y_in), lambda: yv(zz))
    w_q = local(3, ref(q_in), lambda: qv(row))

    def rows_of(z, side):
        return pl.ds(pl.multiple_of((z * 2 + side) * sr, sr), sr)

    def across(s):
        go(f"fw{s}", lambda: tr_in.at[rows_of(s, oh)], lambda: raw.at[oh], (row, s * 2 + h), first, "fw1")

    def along(s):
        go(f"ow{s}", lambda: tr_in.at[rows_of(s, h)], lambda: raw.at[h], (row, s * 2 + h), first, "ow1")

    w_raw = [local(5 + i, lambda i=i: tr_in.at[rows_of(0, i)], lambda i=i: raw.at[i], first) for i in range(2)]
    w_tr = local(7, ref(tr_in), ref(tr))

    pad = LANES - rank
    pg[:, :, rank:, :] = jnp.zeros((n, 2, pad, width), BF16)
    qg[:, rank:, :] = jnp.zeros((n, pad, width), BF16)

    def pad_first():
        q0g[:, rank:, :] = jnp.zeros((n, pad, width), BF16)
    on(rest, pad_first)

    got("px", lambda: pv(oh)(row))
    go("x0", ref(x_in), lambda: xv(zz), xn)
    spread("q1p", "ph", pv(oh))

    def relay(nm, s, view):
        for side, dev, ok, more, slot in (
            ("b", up, zz - s >= 0, (zz - s >= 0) & has_up, lax.rem(zz - s + n, n)),
            ("a", down, zz + s < n, (zz + s < n) & has_down, lax.rem(zz + s, n)),
        ):
            dst = lambda slot=slot: view(slot)
            got(f"{nm}{side}{s}", dst, ok)
            if s + 1 < n:
                go(f"{nm}{side}{s + 1}", dst, dst, dev, more)
            if nm == "x":
                go(f"c{side}{s}", dst, dst, xn, ok)

    spread("q1", "pk", qv, ref(q_in))
    relay("y", 1, yv)
    relay("x", 1, xv)
    go("z1", ref(q_in), lambda: zv(row), up, first)
    across(1)
    second("pg", "pi", pv(h))
    def first_column(cond, more):
        got("z1", lambda: zv(row), cond)
        if more:
            go("z1", lambda: zv(row), lambda: zv(row), up, cond)
        go("zc", lambda: zv(row), lambda: zv(row), near, cond)
        for d, dev in fars:
            go(f"pl{d}", lambda: zv(row), lambda: zv(row), dev, cond)

    half = lambda: c0.at[:, h]

    def relay_core(cond, more):
        got("c0", half, cond)
        if more:
            go("c0", half, half, up, cond)
        go("c0x", half, half, xn, cond)

    for s in range(2, n):
        relay("y", s, yv)
        relay("x", s, xv)
        if s == 2:
            along(1)
            second("ph", "pj", pv(oh))
            first_column(middle, True)
    across(2)
    w_p()
    w_y()
    all_in("p1", "pi", pv(h))
    all_in("q1p", "pj", pv(oh))

    t_at = lax.broadcasted_iota(jnp.int32, (hr, LANES), 0) + h * hr
    u_at = lax.broadcasted_iota(jnp.int32, (hr, LANES), 1)
    nt = (((1,), (1,)), ((), ()))
    tn = (((0,), (0,)), ((), ()))
    for k in range(n):
        value = sum(
            lax.dot_general(yg[k, :, i * width:(i + 1) * width], pg[k, i], nt, preferred_element_type=F32)
            for i in range(2)
        )
        live = (t_at < lr[row, k]) & (u_at < ur[k, zz])
        cb[k, pl.ds(h, 1)] = jnp.where(live, value, 0.0).astype(BF16)[None]
    go("cx", lambda: cb.at[:, h], lambda: cb.at[:, h], xn)
    got("cx", lambda: cb.at[:, oh])

    def keep():
        c0[...] = cb[...]
    on(first, keep)
    go("c0", half, half, up, first)
    relay_core(middle, True)
    for s in range(2, n - 1):
        along(s)
        across(s + 1)
    first_column(last, False)
    second("pk", "pm", qv)

    all_in("q1", "pm", qv)
    w_q()
    w_x()
    got("x0", lambda: xg.at[zz, oh])
    for s in range(1, n):
        got(f"cb{s}", lambda s=s: xg.at[lax.rem(zz - s + n, n), oh], zz - s >= 0)
        got(f"ca{s}", lambda s=s: xg.at[lax.rem(zz + s, n), oh], zz + s < n)
    w_tr()
    step = og.shape[0]
    for at in range(tile // step):
        rows = slice(at * step, (at + 1) * step)
        for k in range(n):
            part = xg[k, :, :, rows].reshape(2 * hr, step)
            og[:, k * LANES:(k + 1) * LANES] = lax.dot_general(
                part, cb[k].reshape(2 * hr, LANES), tn, preferred_element_type=F32).astype(BF16)
        product = jnp.dot(og[...], qg[...].reshape(n * LANES, width), preferred_element_type=F32)
        ub[rows, :] = (tr[rows, :].astype(F32) - product).astype(BF16)
        if at == 0:
            along(n - 1)
    w_up = local(4, ref(ub), ref(up_out))

    relay_core(last, False)
    second("pl", "pn", zv, rest)
    got("c0x", lambda: c0.at[:, oh], rest)
    all_in("zc", "pn", zv, rest)

    def same():
        q0g[...] = qg[...]
    on(first, same)
    blk = og0.shape[0]
    start = zz * 2 * sr
    lanes = pl.ds(pl.multiple_of(start // blk * blk, blk), blk)
    for k in range(n):
        part = xg[k, :, :, lanes].reshape(2 * hr, blk)
        og0[:, k * LANES:(k + 1) * LANES] = lax.dot_general(
            part, c0[k].reshape(2 * hr, LANES), tn, preferred_element_type=F32).astype(BF16)
    prod0[...] = jnp.dot(og0[...], q0g[...].reshape(n * LANES, width), preferred_element_type=F32)

    def finish(side, at):
        inside = pl.ds(pl.multiple_of(lax.rem(start, blk) + side * sr, sr), sr)
        nb[at] = (raw[side].astype(F32) - prod0[inside, :]).astype(BF16)

    def columns(side):
        return np_out.at[:, pl.ds(pl.multiple_of(side * width, width), width)]

    for w in w_raw:
        w()
    got("fw1", lambda: raw.at[oh], rest)
    finish(oh, 0)
    go("pfx", lambda: nb.at[0], lambda: columns(h), xn)
    got("ow1", lambda: raw.at[h], rest)
    finish(h, 1)
    w_np = local(8, lambda: nb.at[1], lambda: columns(h))
    got("pfx", lambda: columns(oh))
    for entry in pending:
        on(*entry[1:])
    w_up()
    w_np()


def body(trailing, left_outer, left_inner, upper_outer, upper_inner, left_ranks, upper_ranks):
    n = lax.axis_size("row")
    nc = lax.axis_size("col")
    tile, width = trailing.shape
    hr = left_outer.shape[0]
    sr = tile // nc
    blk = max(2 * sr, LANES)
    names = sem_names(n, n // 2)
    any_space = pl.BlockSpec(memory_space=pl.ANY)
    smem = pl.BlockSpec(memory_space=pltpu.SMEM)
    vmem = pltpu.VMEM
    return pl.pallas_call(
        functools.partial(kernel, n, names),
        out_shape=(
            jax.ShapeDtypeStruct((tile, width), BF16),
            jax.ShapeDtypeStruct((sr, 2 * width), BF16),
        ),
        in_specs=[any_space] * 5 + [smem] * 2,
        out_specs=(any_space, any_space),
        scratch_shapes=[
            vmem((n, 2, hr, tile), BF16),
            vmem((n, hr, tile), BF16),
            vmem((n, 2, LANES, width), BF16),
            vmem((n, LANES, width), BF16),
            vmem((n, LANES, width), BF16),
            vmem((n, 2, hr, LANES), BF16),
            vmem((n, 2, hr, LANES), BF16),
            vmem((512, n * LANES), BF16),
            vmem((blk, n * LANES), BF16),
            vmem((blk, width), F32),
            vmem((tile, width), BF16),
            vmem((tile, width), BF16),
            vmem((2, sr, width), BF16),
            vmem((2, sr, width), BF16),
            pltpu.SemaphoreType.DMA((len(names),)),
            pltpu.SemaphoreType.DMA((len(names),)),
            pltpu.SemaphoreType.DMA((9,)),
        ],
        compiler_params=pltpu.CompilerParams(
            collective_id=0, has_side_effects=True, vmem_limit_bytes=56 * 2 ** 20
        ),
        cost_estimate=pl.CostEstimate(
            flops=2 * tile * width * n * LANES, bytes_accessed=4 * tile * width, transcendentals=0
        ),
    )(trailing, left_outer, left_inner, upper_outer, upper_inner, left_ranks, upper_ranks)


def solution(mesh):
    in_specs = (
        P("row", "col"),
        P("col", "row"),
        P("col", "row"),
        P("row", "col"),
        P("row", "col"),
        P(),
        P(),
    )
    out_specs = (P("row", "col"), P(("row", "col"), None))
    return jax.shard_map(body, mesh=mesh, in_specs=in_specs, out_specs=out_specs, check_vma=False)
```

```python
import functools

import jax
import jax.numpy as jnp
from jax import lax
from jax.experimental import pallas as pl
from jax.experimental.pallas import tpu as pltpu
from jax.sharding import PartitionSpec as P

MESH = pl.DeviceIdType.MESH
LANES = 128
F32 = jnp.float32
BF16 = jnp.bfloat16


def sem_names(n, nh):
    names = ["px", "x0", "q1", "p1", "q1p", "z1", "zc", "cx", "c0x", "pfx"]
    for s in range(1, n):
        names += [f"xb{s}", f"xa{s}", f"yb{s}", f"ya{s}", f"cb{s}", f"ca{s}"]
        names += [f"fw{s}", f"ow{s}", f"cz{s}"]
    for d in range(1, nh):
        names += [f"p{a}{d}" for a in "ghijklmn"]
    return {name: at for at, name in enumerate(names)}


def kernel(n, names, tr_in, x_in, y_in, p_in, q_in, lr, ur, up_out, np_out,
           xg, yg, pg, qg, q0g, cb, c0, og, og0, prod0, tr, ub, raw, nb,
           ssem, rsem, lsem):
    nh = n // 2
    rank = p_in.shape[0]
    hr = x_in.shape[0]
    tile, width = tr_in.shape
    sr = np_out.shape[0]
    row, col = lax.axis_index("row"), lax.axis_index("col")
    zz, h = col // 2, col % 2
    oh = 1 - h
    hi, core = row // 2, row % 2
    mate = hi * 2 + (1 - core)
    xn = (row, zz * 2 + oh)
    up = (row, lax.rem(zz + 1, n) * 2 + h)
    down = (row, lax.rem(zz + n - 1, n) * 2 + h)
    first, rest = zz == 0, zz > 0
    has_up, has_down = zz < n - 1, zz > 0
    pending = []

    def on(cond, f):
        if cond is None:
            f()
        else:
            pl.when(cond)(f)

    def desc(name, src, dst, dev):
        at = names[name]
        return pltpu.make_async_remote_copy(
            src_ref=src(), dst_ref=dst(), send_sem=ssem.at[at], recv_sem=rsem.at[at],
            device_id=dev, device_id_type=MESH)

    def go(name, src, dst, dev, cond=None, sem=None):
        def make():
            at = names[sem or name]
            return pltpu.make_async_remote_copy(
                src_ref=src(), dst_ref=dst(), send_sem=ssem.at[names[name]],
                recv_sem=rsem.at[at], device_id=dev, device_id_type=MESH)
        on(cond, lambda: make().start())
        pending.append((name, cond, lambda: make().wait_send()))

    def got(name, dst, cond=None):
        on(cond, lambda: desc(name, dst, dst, xn).wait_recv())

    def local(at, src, dst, cond=None):
        def make():
            return pltpu.make_async_copy(src(), dst(), lsem.at[at])
        on(cond, lambda: make().start())
        return lambda: on(cond, lambda: make().wait())

    partners = [xn, (mate, col)]
    for s in range(1, n):
        partners.append((row, lax.rem(zz + s, n) * 2 + h))
    for d in range(1, nh):
        partners.append((lax.rem(hi + d, nh) * 2 + core, col))
    barrier = pltpu.get_barrier_semaphore()
    for dev in partners:
        pl.semaphore_signal(barrier, inc=1, device_id=dev, device_id_type=MESH)
    pl.semaphore_wait(barrier, len(partners))

    def ref(r):
        return lambda: r

    pd = pl.ds(0, rank)
    fars = [(d, (lax.rem(hi + d, nh) * 2 + core, col)) for d in range(1, nh)]
    near = (mate, col)
    middle, last = rest & has_up, zz == n - 1
    yv, xv = (lambda k: yg.at[k]), (lambda k: xg.at[k, h])
    pv = lambda side: lambda k: pg.at[k, side, pd]
    qv, zv = (lambda k: qg.at[k, pd]), (lambda k: q0g.at[k, pd])

    def spread(near_name, far_name, view, src=None):
        src = src or (lambda: view(row))
        go(near_name, src, lambda: view(row), near)
        for d, dev in fars:
            go(f"{far_name}{d}", src, lambda: view(row), dev)

    def far(d):
        return lax.rem(hi + nh - d, nh) * 2 + core

    def far_mate(d):
        return lax.rem(hi + nh - d, nh) * 2 + 1 - core

    def second(first_name, second_name, view, cond=None):
        for d in range(1, nh):
            got(f"{first_name}{d}", lambda d=d: view(far(d)), cond)
            go(f"{second_name}{d}", lambda d=d: view(far(d)), lambda d=d: view(far(d)), near, cond)

    def all_in(near_name, second_name, view, cond=None):
        got(near_name, lambda: view(mate), cond)
        for d in range(1, nh):
            got(f"{second_name}{d}", lambda d=d: view(far_mate(d)), cond)

    go("yb1", ref(y_in), lambda: yv(zz), up, has_up)
    go("ya1", ref(y_in), lambda: yv(zz), down, has_down)
    go("xb1", ref(x_in), lambda: xv(zz), up, has_up)
    go("xa1", ref(x_in), lambda: xv(zz), down, has_down)
    go("px", ref(p_in), lambda: pv(h)(row), xn)
    spread("p1", "pg", pv(h), ref(p_in))
    w_p = local(0, ref(p_in), lambda: pv(h)(row))
    w_x = local(1, ref(x_in), lambda: xv(zz))
    w_y = local(2, ref(y_in), lambda: yv(zz))
    w_q = local(3, ref(q_in), lambda: qv(row))

    def rows_of(z, side):
        return pl.ds(pl.multiple_of((z * 2 + side) * sr, sr), sr)

    def across(s):
        go(f"fw{s}", lambda: tr_in.at[rows_of(s, oh)], lambda: raw.at[oh], (row, s * 2 + h), first, "fw1")

    def along(s):
        go(f"ow{s}", lambda: tr_in.at[rows_of(s, h)], lambda: raw.at[h], (row, s * 2 + h), first, "ow1")

    w_raw = [local(5 + i, lambda i=i: tr_in.at[rows_of(0, i)], lambda i=i: raw.at[i], first) for i in range(2)]
    w_tr = local(7, ref(tr_in), ref(tr))

    pad = LANES - rank
    pg[:, :, rank:, :] = jnp.zeros((n, 2, pad, width), BF16)
    qg[:, rank:, :] = jnp.zeros((n, pad, width), BF16)

    def pad_first():
        q0g[:, rank:, :] = jnp.zeros((n, pad, width), BF16)
    on(rest, pad_first)

    got("px", lambda: pv(oh)(row))
    go("x0", ref(x_in), lambda: xv(zz), xn)
    spread("q1p", "ph", pv(oh))

    def relay(nm, s, view):
        for side, dev, ok, more, slot in (
            ("b", up, zz - s >= 0, (zz - s >= 0) & has_up, lax.rem(zz - s + n, n)),
            ("a", down, zz + s < n, (zz + s < n) & has_down, lax.rem(zz + s, n)),
        ):
            dst = lambda slot=slot: view(slot)
            got(f"{nm}{side}{s}", dst, ok)
            if s + 1 < n:
                go(f"{nm}{side}{s + 1}", dst, dst, dev, more)
            if nm == "x":
                go(f"c{side}{s}", dst, dst, xn, ok)

    spread("q1", "pk", qv, ref(q_in))
    relay("y", 1, yv)
    relay("x", 1, xv)
    go("z1", ref(q_in), lambda: zv(row), up, first)
    across(1)
    second("pg", "pi", pv(h))
    def first_column(cond, more):
        got("z1", lambda: zv(row), cond)
        if more:
            go("z1", lambda: zv(row), lambda: zv(row), up, cond)
        go("zc", lambda: zv(row), lambda: zv(row), near, cond)
        for d, dev in fars:
            go(f"pl{d}", lambda: zv(row), lambda: zv(row), dev, cond)

    half = lambda: c0.at[:, h]

    for s in range(2, n):
        relay("y", s, yv)
        relay("x", s, xv)
        if s == 2:
            along(1)
            second("ph", "pj", pv(oh))
            first_column(middle, True)
    w_p()
    w_y()
    all_in("p1", "pi", pv(h))
    all_in("q1p", "pj", pv(oh))

    t_at = lax.broadcasted_iota(jnp.int32, (hr, LANES), 0) + h * hr
    u_at = lax.broadcasted_iota(jnp.int32, (hr, LANES), 1)
    nt = (((1,), (1,)), ((), ()))
    tn = (((0,), (0,)), ((), ()))
    for k in range(n):
        value = sum(
            lax.dot_general(yg[k, :, i * width:(i + 1) * width], pg[k, i], nt, preferred_element_type=F32)
            for i in range(2)
        )
        live = (t_at < lr[row, k]) & (u_at < ur[k, zz])
        cb[k, pl.ds(h, 1)] = jnp.where(live, value, 0.0).astype(BF16)[None]
    go("cx", lambda: cb.at[:, h], lambda: cb.at[:, h], xn)
    got("cx", lambda: cb.at[:, oh])

    def keep():
        c0[...] = cb[...]
    on(first, keep)
    for s in range(n - 1, 0, -1):
        go(f"cz{s}", half, half, (row, s * 2 + h), first, "cz1")
    for s in range(2, n):
        across(s)
        if s < n - 1:
            along(s)
    first_column(last, False)
    second("pk", "pm", qv)
    got("cz1", half, rest)
    go("c0x", half, half, xn, rest)
    second("pl", "pn", zv, rest)

    all_in("q1", "pm", qv)
    w_q()
    w_x()
    got("x0", lambda: xg.at[zz, oh])
    for s in range(1, n):
        got(f"cb{s}", lambda s=s: xg.at[lax.rem(zz - s + n, n), oh], zz - s >= 0)
        got(f"ca{s}", lambda s=s: xg.at[lax.rem(zz + s, n), oh], zz + s < n)
    w_tr()
    step = og.shape[0]
    for at in range(tile // step):
        rows = slice(at * step, (at + 1) * step)
        for k in range(n):
            part = xg[k, :, :, rows].reshape(2 * hr, step)
            og[:, k * LANES:(k + 1) * LANES] = lax.dot_general(
                part, cb[k].reshape(2 * hr, LANES), tn, preferred_element_type=F32).astype(BF16)
        product = jnp.dot(og[...], qg[...].reshape(n * LANES, width), preferred_element_type=F32)
        ub[rows, :] = (tr[rows, :].astype(F32) - product).astype(BF16)
        if at == 0:
            along(n - 1)
    w_up = local(4, ref(ub), ref(up_out))

    got("c0x", lambda: c0.at[:, oh], rest)
    all_in("zc", "pn", zv, rest)

    def same():
        q0g[...] = qg[...]
    on(first, same)
    blk = og0.shape[0]
    start = zz * 2 * sr
    lanes = pl.ds(pl.multiple_of(start // blk * blk, blk), blk)
    for k in range(n):
        part = xg[k, :, :, lanes].reshape(2 * hr, blk)
        og0[:, k * LANES:(k + 1) * LANES] = lax.dot_general(
            part, c0[k].reshape(2 * hr, LANES), tn, preferred_element_type=F32).astype(BF16)
    prod0[...] = jnp.dot(og0[...], q0g[...].reshape(n * LANES, width), preferred_element_type=F32)

    def finish(side, at):
        inside = pl.ds(pl.multiple_of(lax.rem(start, blk) + side * sr, sr), sr)
        nb[at] = (raw[side].astype(F32) - prod0[inside, :]).astype(BF16)

    def columns(side):
        return np_out.at[:, pl.ds(pl.multiple_of(side * width, width), width)]

    for w in w_raw:
        w()
    got("fw1", lambda: raw.at[oh], rest)
    finish(oh, 0)
    go("pfx", lambda: nb.at[0], lambda: columns(h), xn)
    got("ow1", lambda: raw.at[h], rest)
    finish(h, 1)
    w_np = local(8, lambda: nb.at[1], lambda: columns(h))
    got("pfx", lambda: columns(oh))
    for entry in pending:
        on(*entry[1:])
    w_up()
    w_np()


def body(trailing, left_outer, left_inner, upper_outer, upper_inner, left_ranks, upper_ranks):
    n = lax.axis_size("row")
    nc = lax.axis_size("col")
    tile, width = trailing.shape
    hr = left_outer.shape[0]
    sr = tile // nc
    blk = max(2 * sr, LANES)
    names = sem_names(n, n // 2)
    any_space = pl.BlockSpec(memory_space=pl.ANY)
    smem = pl.BlockSpec(memory_space=pltpu.SMEM)
    vmem = pltpu.VMEM
    return pl.pallas_call(
        functools.partial(kernel, n, names),
        out_shape=(
            jax.ShapeDtypeStruct((tile, width), BF16),
            jax.ShapeDtypeStruct((sr, 2 * width), BF16),
        ),
        in_specs=[any_space] * 5 + [smem] * 2,
        out_specs=(any_space, any_space),
        scratch_shapes=[
            vmem((n, 2, hr, tile), BF16),
            vmem((n, hr, tile), BF16),
            vmem((n, 2, LANES, width), BF16),
            vmem((n, LANES, width), BF16),
            vmem((n, LANES, width), BF16),
            vmem((n, 2, hr, LANES), BF16),
            vmem((n, 2, hr, LANES), BF16),
            vmem((512, n * LANES), BF16),
            vmem((blk, n * LANES), BF16),
            vmem((blk, width), F32),
            vmem((tile, width), BF16),
            vmem((tile, width), BF16),
            vmem((2, sr, width), BF16),
            vmem((2, sr, width), BF16),
            pltpu.SemaphoreType.DMA((len(names),)),
            pltpu.SemaphoreType.DMA((len(names),)),
            pltpu.SemaphoreType.DMA((9,)),
        ],
        compiler_params=pltpu.CompilerParams(
            collective_id=0, has_side_effects=True, vmem_limit_bytes=56 * 2 ** 20
        ),
        cost_estimate=pl.CostEstimate(
            flops=2 * tile * width * n * LANES, bytes_accessed=4 * tile * width, transcendentals=0
        ),
    )(trailing, left_outer, left_inner, upper_outer, upper_inner, left_ranks, upper_ranks)


def solution(mesh):
    in_specs = (
        P("row", "col"),
        P("col", "row"),
        P("col", "row"),
        P("row", "col"),
        P("row", "col"),
        P(),
        P(),
    )
    out_specs = (P("row", "col"), P(("row", "col"), None))
    return jax.shard_map(body, mesh=mesh, in_specs=in_specs, out_specs=out_specs, check_vma=False)
```

```python
import functools

import jax
import jax.numpy as jnp
from jax import lax
from jax.experimental import pallas as pl
from jax.experimental.pallas import tpu as pltpu
from jax.sharding import PartitionSpec as P

MESH = pl.DeviceIdType.MESH
LANES = 128
F32 = jnp.float32
BF16 = jnp.bfloat16


def sem_names(n, nh):
    names = ["px", "x0", "q1", "p1", "q1p", "z1", "zc", "cx", "c0x", "pfx"]
    for s in range(1, n):
        names += [f"xb{s}", f"xa{s}", f"yb{s}", f"ya{s}", f"cb{s}", f"ca{s}"]
        names += [f"fw{s}", f"ow{s}", f"cz{s}"]
    for d in range(1, nh):
        names += [f"p{a}{d}" for a in "ghijklmn"]
    return {name: at for at, name in enumerate(names)}


def kernel(n, names, tr_in, x_in, y_in, p_in, q_in, lr, ur, up_out, np_out,
           xg, yg, pg, qg, q0g, cb, c0, og, og0, prod0, tr, ub, raw, nb,
           ssem, rsem, lsem):
    nh = n // 2
    rank = p_in.shape[0]
    hr = x_in.shape[0]
    tile, width = tr_in.shape
    sr = np_out.shape[0]
    row, col = lax.axis_index("row"), lax.axis_index("col")
    zz, h = col // 2, col % 2
    oh = 1 - h
    hi, core = row // 2, row % 2
    mate = hi * 2 + (1 - core)
    xn = (row, zz * 2 + oh)
    up = (row, lax.rem(zz + 1, n) * 2 + h)
    down = (row, lax.rem(zz + n - 1, n) * 2 + h)
    first, rest = zz == 0, zz > 0
    has_up, has_down = zz < n - 1, zz > 0
    pending = []

    def on(cond, f):
        if cond is None:
            f()
        else:
            pl.when(cond)(f)

    def desc(name, src, dst, dev):
        at = names[name]
        return pltpu.make_async_remote_copy(
            src_ref=src(), dst_ref=dst(), send_sem=ssem.at[at], recv_sem=rsem.at[at],
            device_id=dev, device_id_type=MESH)

    def go(name, src, dst, dev, cond=None, sem=None):
        def make():
            at = names[sem or name]
            return pltpu.make_async_remote_copy(
                src_ref=src(), dst_ref=dst(), send_sem=ssem.at[names[name]],
                recv_sem=rsem.at[at], device_id=dev, device_id_type=MESH)
        on(cond, lambda: make().start())
        pending.append((name, cond, lambda: make().wait_send()))

    def got(name, dst, cond=None):
        on(cond, lambda: desc(name, dst, dst, xn).wait_recv())

    def local(at, src, dst, cond=None):
        def make():
            return pltpu.make_async_copy(src(), dst(), lsem.at[at])
        on(cond, lambda: make().start())
        return lambda: on(cond, lambda: make().wait())

    partners = [xn, (mate, col)]
    for s in range(1, n):
        partners.append((row, lax.rem(zz + s, n) * 2 + h))
    for d in range(1, nh):
        partners.append((lax.rem(hi + d, nh) * 2 + core, col))
    barrier = pltpu.get_barrier_semaphore()
    for dev in partners:
        pl.semaphore_signal(barrier, inc=1, device_id=dev, device_id_type=MESH)
    pl.semaphore_wait(barrier, len(partners))

    def ref(r):
        return lambda: r

    pd = pl.ds(0, rank)
    fars = [(d, (lax.rem(hi + d, nh) * 2 + core, col)) for d in range(1, nh)]
    near = (mate, col)
    middle, last = rest & has_up, zz == n - 1
    yv, xv = (lambda k: yg.at[k]), (lambda k: xg.at[k, h])
    pv = lambda side: lambda k: pg.at[k, side, pd]
    qv, zv = (lambda k: qg.at[k, pd]), (lambda k: q0g.at[k, pd])

    def spread(near_name, far_name, view, src=None):
        src = src or (lambda: view(row))
        go(near_name, src, lambda: view(row), near)
        for d, dev in fars:
            go(f"{far_name}{d}", src, lambda: view(row), dev)

    def far(d):
        return lax.rem(hi + nh - d, nh) * 2 + core

    def far_mate(d):
        return lax.rem(hi + nh - d, nh) * 2 + 1 - core

    def second(first_name, second_name, view, cond=None):
        for d in range(1, nh):
            got(f"{first_name}{d}", lambda d=d: view(far(d)), cond)
            go(f"{second_name}{d}", lambda d=d: view(far(d)), lambda d=d: view(far(d)), near, cond)

    def all_in(near_name, second_name, view, cond=None):
        got(near_name, lambda: view(mate), cond)
        for d in range(1, nh):
            got(f"{second_name}{d}", lambda d=d: view(far_mate(d)), cond)

    go("yb1", ref(y_in), lambda: yv(zz), up, has_up)
    go("ya1", ref(y_in), lambda: yv(zz), down, has_down)
    go("xb1", ref(x_in), lambda: xv(zz), up, has_up)
    go("xa1", ref(x_in), lambda: xv(zz), down, has_down)
    go("px", ref(p_in), lambda: pv(h)(row), xn)
    spread("p1", "pg", pv(h), ref(p_in))
    w_p = local(0, ref(p_in), lambda: pv(h)(row))
    w_x = local(1, ref(x_in), lambda: xv(zz))
    w_y = local(2, ref(y_in), lambda: yv(zz))
    w_q = local(3, ref(q_in), lambda: qv(row))

    def rows_of(z, side):
        return pl.ds(pl.multiple_of((z * 2 + side) * sr, sr), sr)

    def across(s):
        go(f"fw{s}", lambda: tr_in.at[rows_of(s, oh)], lambda: raw.at[oh], (row, s * 2 + h), first, "fw1")

    def along(s):
        go(f"ow{s}", lambda: tr_in.at[rows_of(s, h)], lambda: raw.at[h], (row, s * 2 + h), first, "ow1")

    w_raw = [local(5 + i, lambda i=i: tr_in.at[rows_of(0, i)], lambda i=i: raw.at[i], first) for i in range(2)]
    w_tr = local(7, ref(tr_in), ref(tr))

    pad = LANES - rank
    pg[:, :, rank:, :] = jnp.zeros((n, 2, pad, width), BF16)
    qg[:, rank:, :] = jnp.zeros((n, pad, width), BF16)

    def pad_first():
        q0g[:, rank:, :] = jnp.zeros((n, pad, width), BF16)
    on(rest, pad_first)

    got("px", lambda: pv(oh)(row))
    go("x0", ref(x_in), lambda: xv(zz), xn)
    spread("q1p", "ph", pv(oh))

    def relay(nm, s, view):
        for side, dev, ok, more, slot in (
            ("b", up, zz - s >= 0, (zz - s >= 0) & has_up, lax.rem(zz - s + n, n)),
            ("a", down, zz + s < n, (zz + s < n) & has_down, lax.rem(zz + s, n)),
        ):
            dst = lambda slot=slot: view(slot)
            got(f"{nm}{side}{s}", dst, ok)
            if s + 1 < n:
                go(f"{nm}{side}{s + 1}", dst, dst, dev, more)
            if nm == "x":
                go(f"c{side}{s}", dst, dst, xn, ok)

    spread("q1", "pk", qv, ref(q_in))
    relay("y", 1, yv)
    relay("x", 1, xv)
    go("z1", ref(q_in), lambda: zv(row), up, first)
    across(1)
    second("pg", "pi", pv(h))
    def first_column(cond, more):
        got("z1", lambda: zv(row), cond)
        if more:
            go("z1", lambda: zv(row), lambda: zv(row), up, cond)
        go("zc", lambda: zv(row), lambda: zv(row), near, cond)
        for d, dev in fars:
            go(f"pl{d}", lambda: zv(row), lambda: zv(row), dev, cond)

    half = lambda: c0.at[:, h]

    for s in range(2, n):
        relay("y", s, yv)
        relay("x", s, xv)
        if s == 2:
            along(1)
            second("ph", "pj", pv(oh))
            first_column(middle, True)
            across(2)
    w_p()
    w_y()
    all_in("p1", "pi", pv(h))
    all_in("q1p", "pj", pv(oh))

    t_at = lax.broadcasted_iota(jnp.int32, (hr, LANES), 0) + h * hr
    u_at = lax.broadcasted_iota(jnp.int32, (hr, LANES), 1)
    nt = (((1,), (1,)), ((), ()))
    tn = (((0,), (0,)), ((), ()))
    for k in range(n):
        value = sum(
            lax.dot_general(yg[k, :, i * width:(i + 1) * width], pg[k, i], nt, preferred_element_type=F32)
            for i in range(2)
        )
        live = (t_at < lr[row, k]) & (u_at < ur[k, zz])
        cb[k, pl.ds(h, 1)] = jnp.where(live, value, 0.0).astype(BF16)[None]
    go("cx", lambda: cb.at[:, h], lambda: cb.at[:, h], xn)
    got("cx", lambda: cb.at[:, oh])

    def keep():
        c0[...] = cb[...]
    on(first, keep)
    for s in range(n - 1, 0, -1):
        go(f"cz{s}", half, half, (row, s * 2 + h), first, "cz1")
    for s in range(2, n - 1):
        along(s)
        across(s + 1)
    first_column(last, False)
    second("pk", "pm", qv)
    got("cz1", half, rest)
    go("c0x", half, half, xn, rest)
    second("pl", "pn", zv, rest)

    all_in("q1", "pm", qv)
    w_q()
    w_x()
    got("x0", lambda: xg.at[zz, oh])
    for s in range(1, n):
        got(f"cb{s}", lambda s=s: xg.at[lax.rem(zz - s + n, n), oh], zz - s >= 0)
        got(f"ca{s}", lambda s=s: xg.at[lax.rem(zz + s, n), oh], zz + s < n)
    w_tr()
    step = og.shape[0]
    for at in range(tile // step):
        rows = slice(at * step, (at + 1) * step)
        for k in range(n):
            part = xg[k, :, :, rows].reshape(2 * hr, step)
            og[:, k * LANES:(k + 1) * LANES] = lax.dot_general(
                part, cb[k].reshape(2 * hr, LANES), tn, preferred_element_type=F32).astype(BF16)
        product = jnp.dot(og[...], qg[...].reshape(n * LANES, width), preferred_element_type=F32)
        ub[rows, :] = (tr[rows, :].astype(F32) - product).astype(BF16)
        if at == 0:
            along(n - 1)
    w_up = local(4, ref(ub), ref(up_out))

    got("c0x", lambda: c0.at[:, oh], rest)
    all_in("zc", "pn", zv, rest)

    def same():
        q0g[...] = qg[...]
    on(first, same)
    blk = og0.shape[0]
    start = zz * 2 * sr
    lanes = pl.ds(pl.multiple_of(start // blk * blk, blk), blk)
    for k in range(n):
        part = xg[k, :, :, lanes].reshape(2 * hr, blk)
        og0[:, k * LANES:(k + 1) * LANES] = lax.dot_general(
            part, c0[k].reshape(2 * hr, LANES), tn, preferred_element_type=F32).astype(BF16)
    prod0[...] = jnp.dot(og0[...], q0g[...].reshape(n * LANES, width), preferred_element_type=F32)

    def finish(side, at):
        inside = pl.ds(pl.multiple_of(lax.rem(start, blk) + side * sr, sr), sr)
        nb[at] = (raw[side].astype(F32) - prod0[inside, :]).astype(BF16)

    def columns(side):
        return np_out.at[:, pl.ds(pl.multiple_of(side * width, width), width)]

    for w in w_raw:
        w()
    got("fw1", lambda: raw.at[oh], rest)
    finish(oh, 0)
    go("pfx", lambda: nb.at[0], lambda: columns(h), xn)
    got("ow1", lambda: raw.at[h], rest)
    finish(h, 1)
    w_np = local(8, lambda: nb.at[1], lambda: columns(h))
    got("pfx", lambda: columns(oh))
    for entry in pending:
        on(*entry[1:])
    w_up()
    w_np()


def hand_on(u_in, p_in, u_out, p_out, sems):
    parts = sems.shape[0] - 1
    size = u_in.shape[0] // parts
    copies = [pltpu.make_async_copy(p_in, p_out, sems.at[parts])]
    for i in range(parts):
        rows = pl.ds(i * size, size)
        copies.append(pltpu.make_async_copy(u_in.at[rows], u_out.at[rows], sems.at[i]))
    for c in copies:
        c.start()
    for c in copies:
        c.wait()


def body(trailing, left_outer, left_inner, upper_outer, upper_inner, left_ranks, upper_ranks):
    n = lax.axis_size("row")
    nc = lax.axis_size("col")
    tile, width = trailing.shape
    hr = left_outer.shape[0]
    sr = tile // nc
    blk = max(2 * sr, LANES)
    names = sem_names(n, n // 2)
    any_space = pl.BlockSpec(memory_space=pl.ANY)
    smem = pl.BlockSpec(memory_space=pltpu.SMEM)
    vmem = pltpu.VMEM
    shapes = (
        jax.ShapeDtypeStruct((tile, width), BF16),
        jax.ShapeDtypeStruct((sr, 2 * width), BF16),
    )
    results = pl.pallas_call(
        functools.partial(kernel, n, names),
        out_shape=shapes,
        in_specs=[any_space] * 5 + [smem] * 2,
        out_specs=(any_space, any_space),
        scratch_shapes=[
            vmem((n, 2, hr, tile), BF16),
            vmem((n, hr, tile), BF16),
            vmem((n, 2, LANES, width), BF16),
            vmem((n, LANES, width), BF16),
            vmem((n, LANES, width), BF16),
            vmem((n, 2, hr, LANES), BF16),
            vmem((n, 2, hr, LANES), BF16),
            vmem((512, n * LANES), BF16),
            vmem((blk, n * LANES), BF16),
            vmem((blk, width), F32),
            vmem((tile, width), BF16),
            vmem((tile, width), BF16),
            vmem((2, sr, width), BF16),
            vmem((2, sr, width), BF16),
            pltpu.SemaphoreType.DMA((len(names),)),
            pltpu.SemaphoreType.DMA((len(names),)),
            pltpu.SemaphoreType.DMA((9,)),
        ],
        compiler_params=pltpu.CompilerParams(
            collective_id=0, has_side_effects=True, vmem_limit_bytes=56 * 2 ** 20
        ),
        cost_estimate=pl.CostEstimate(
            flops=2 * tile * width * n * LANES, bytes_accessed=4 * tile * width, transcendentals=0
        ),
    )(trailing, left_outer, left_inner, upper_outer, upper_inner, left_ranks, upper_ranks)
    return pl.pallas_call(
        hand_on,
        out_shape=shapes,
        in_specs=[any_space] * 2,
        out_specs=(any_space, any_space),
        scratch_shapes=[pltpu.SemaphoreType.DMA((9,))],
        compiler_params=pltpu.CompilerParams(vmem_limit_bytes=56 * 2 ** 20),
    )(*results)


def solution(mesh):
    in_specs = (
        P("row", "col"),
        P("col", "row"),
        P("col", "row"),
        P("row", "col"),
        P("row", "col"),
        P(),
        P(),
    )
    out_specs = (P("row", "col"), P(("row", "col"), None))
    return jax.shard_map(body, mesh=mesh, in_specs=in_specs, out_specs=out_specs, check_vma=False)
```

```python
import functools

import jax
import jax.numpy as jnp
from jax import lax
from jax.experimental import pallas as pl
from jax.experimental.pallas import tpu as pltpu
from jax.sharding import PartitionSpec as P

MESH = pl.DeviceIdType.MESH
LANES = 128
F32 = jnp.float32
BF16 = jnp.bfloat16


def sem_names(n, nh):
    names = ["px", "x0", "q1", "p1", "q1p", "z1", "zc", "cx", "c0x", "pfx"]
    for s in range(1, n):
        names += [f"xb{s}", f"xa{s}", f"yb{s}", f"ya{s}", f"cb{s}", f"ca{s}"]
        names += [f"fw{s}", f"ow{s}", f"cz{s}"]
    for d in range(1, nh):
        names += [f"p{a}{d}" for a in "ghijklmn"]
    return {name: at for at, name in enumerate(names)}


def kernel(n, names, tr_in, x_in, y_in, p_in, q_in, lr, ur, up_out, np_out,
           xg, yg, pg, qg, q0g, cb, c0, og, og0, prod0, tr, ub, raw, nb,
           ssem, rsem, lsem):
    nh = n // 2
    rank = p_in.shape[0]
    hr = x_in.shape[0]
    tile, width = tr_in.shape
    sr = np_out.shape[0]
    row, col = lax.axis_index("row"), lax.axis_index("col")
    zz, h = col // 2, col % 2
    oh = 1 - h
    hi, core = row // 2, row % 2
    mate = hi * 2 + (1 - core)
    xn = (row, zz * 2 + oh)
    up = (row, lax.rem(zz + 1, n) * 2 + h)
    down = (row, lax.rem(zz + n - 1, n) * 2 + h)
    first, rest = zz == 0, zz > 0
    has_up, has_down = zz < n - 1, zz > 0
    pending = []

    def on(cond, f):
        if cond is None:
            f()
        else:
            pl.when(cond)(f)

    def desc(name, src, dst, dev):
        at = names[name]
        return pltpu.make_async_remote_copy(
            src_ref=src(), dst_ref=dst(), send_sem=ssem.at[at], recv_sem=rsem.at[at],
            device_id=dev, device_id_type=MESH)

    def go(name, src, dst, dev, cond=None, sem=None):
        def make():
            at = names[sem or name]
            return pltpu.make_async_remote_copy(
                src_ref=src(), dst_ref=dst(), send_sem=ssem.at[names[name]],
                recv_sem=rsem.at[at], device_id=dev, device_id_type=MESH)
        on(cond, lambda: make().start())
        pending.append((name, cond, lambda: make().wait_send()))

    def got(name, dst, cond=None):
        on(cond, lambda: desc(name, dst, dst, xn).wait_recv())

    def local(at, src, dst, cond=None):
        def make():
            return pltpu.make_async_copy(src(), dst(), lsem.at[at])
        on(cond, lambda: make().start())
        return lambda: on(cond, lambda: make().wait())

    partners = [xn, (mate, col)]
    for s in range(1, n):
        partners.append((row, lax.rem(zz + s, n) * 2 + h))
    for d in range(1, nh):
        partners.append((lax.rem(hi + d, nh) * 2 + core, col))
    barrier = pltpu.get_barrier_semaphore()
    for dev in partners:
        pl.semaphore_signal(barrier, inc=1, device_id=dev, device_id_type=MESH)
    pl.semaphore_wait(barrier, len(partners))

    def ref(r):
        return lambda: r

    pd = pl.ds(0, rank)
    fars = [(d, (lax.rem(hi + d, nh) * 2 + core, col)) for d in range(1, nh)]
    near = (mate, col)
    middle, last = rest & has_up, zz == n - 1
    yv, xv = (lambda k: yg.at[k]), (lambda k: xg.at[k, h])
    pv = lambda side: lambda k: pg.at[k, side, pd]
    qv, zv = (lambda k: qg.at[k, pd]), (lambda k: q0g.at[k, pd])

    def spread(near_name, far_name, view, src=None):
        src = src or (lambda: view(row))
        go(near_name, src, lambda: view(row), near)
        for d, dev in fars:
            go(f"{far_name}{d}", src, lambda: view(row), dev)

    def far(d):
        return lax.rem(hi + nh - d, nh) * 2 + core

    def far_mate(d):
        return lax.rem(hi + nh - d, nh) * 2 + 1 - core

    def second(first_name, second_name, view, cond=None):
        for d in range(1, nh):
            got(f"{first_name}{d}", lambda d=d: view(far(d)), cond)
            go(f"{second_name}{d}", lambda d=d: view(far(d)), lambda d=d: view(far(d)), near, cond)

    def all_in(near_name, second_name, view, cond=None):
        got(near_name, lambda: view(mate), cond)
        for d in range(1, nh):
            got(f"{second_name}{d}", lambda d=d: view(far_mate(d)), cond)

    go("yb1", ref(y_in), lambda: yv(zz), up, has_up)
    go("ya1", ref(y_in), lambda: yv(zz), down, has_down)
    go("xb1", ref(x_in), lambda: xv(zz), up, has_up)
    go("xa1", ref(x_in), lambda: xv(zz), down, has_down)
    go("px", ref(p_in), lambda: pv(h)(row), xn)
    spread("p1", "pg", pv(h), ref(p_in))
    w_p = local(0, ref(p_in), lambda: pv(h)(row))
    w_x = local(1, ref(x_in), lambda: xv(zz))
    w_y = local(2, ref(y_in), lambda: yv(zz))
    w_q = local(3, ref(q_in), lambda: qv(row))

    def rows_of(z, side):
        return pl.ds(pl.multiple_of((z * 2 + side) * sr, sr), sr)

    def across(s):
        go(f"fw{s}", lambda: tr_in.at[rows_of(s, oh)], lambda: raw.at[oh], (row, s * 2 + h), first, "fw1")

    def along(s):
        go(f"ow{s}", lambda: tr_in.at[rows_of(s, h)], lambda: raw.at[h], (row, s * 2 + h), first, "ow1")

    w_raw = [local(5 + i, lambda i=i: tr_in.at[rows_of(0, i)], lambda i=i: raw.at[i], first) for i in range(2)]
    w_tr = local(7, ref(tr_in), ref(tr))

    pad = LANES - rank
    pg[:, :, rank:, :] = jnp.zeros((n, 2, pad, width), BF16)
    qg[:, rank:, :] = jnp.zeros((n, pad, width), BF16)

    def pad_first():
        q0g[:, rank:, :] = jnp.zeros((n, pad, width), BF16)
    on(rest, pad_first)

    got("px", lambda: pv(oh)(row))
    go("x0", ref(x_in), lambda: xv(zz), xn)
    spread("q1p", "ph", pv(oh))

    def relay(nm, s, view):
        for side, dev, ok, more, slot in (
            ("b", up, zz - s >= 0, (zz - s >= 0) & has_up, lax.rem(zz - s + n, n)),
            ("a", down, zz + s < n, (zz + s < n) & has_down, lax.rem(zz + s, n)),
        ):
            dst = lambda slot=slot: view(slot)
            got(f"{nm}{side}{s}", dst, ok)
            if s + 1 < n:
                go(f"{nm}{side}{s + 1}", dst, dst, dev, more)
            if nm == "x":
                go(f"c{side}{s}", dst, dst, xn, ok)

    spread("q1", "pk", qv, ref(q_in))
    relay("y", 1, yv)
    relay("x", 1, xv)
    go("z1", ref(q_in), lambda: zv(row), up, first)
    across(1)
    second("pg", "pi", pv(h))
    def first_column(cond, more):
        got("z1", lambda: zv(row), cond)
        if more:
            go("z1", lambda: zv(row), lambda: zv(row), up, cond)
        go("zc", lambda: zv(row), lambda: zv(row), near, cond)
        for d, dev in fars:
            go(f"pl{d}", lambda: zv(row), lambda: zv(row), dev, cond)

    half = lambda: c0.at[:, h]

    for s in range(2, n):
        relay("y", s, yv)
        relay("x", s, xv)
        if s == 2:
            along(1)
            second("ph", "pj", pv(oh))
            first_column(middle, True)
            across(2)
    w_p()
    w_y()
    all_in("p1", "pi", pv(h))
    all_in("q1p", "pj", pv(oh))

    t_at = lax.broadcasted_iota(jnp.int32, (hr, LANES), 0) + h * hr
    u_at = lax.broadcasted_iota(jnp.int32, (hr, LANES), 1)
    nt = (((1,), (1,)), ((), ()))
    tn = (((0,), (0,)), ((), ()))
    for k in range(n):
        value = sum(
            lax.dot_general(yg[k, :, i * width:(i + 1) * width], pg[k, i], nt, preferred_element_type=F32)
            for i in range(2)
        )
        live = (t_at < lr[row, k]) & (u_at < ur[k, zz])
        cb[k, pl.ds(h, 1)] = jnp.where(live, value, 0.0).astype(BF16)[None]
    go("cx", lambda: cb.at[:, h], lambda: cb.at[:, h], xn)
    got("cx", lambda: cb.at[:, oh])

    def keep():
        c0[...] = cb[...]
    on(first, keep)
    for s in range(n - 1, 0, -1):
        go(f"cz{s}", half, half, (row, s * 2 + h), first, "cz1")
    for s in range(2, n - 1):
        along(s)
        across(s + 1)
    first_column(last, False)
    second("pk", "pm", qv)
    got("cz1", half, rest)
    go("c0x", half, half, xn, rest)
    second("pl", "pn", zv, rest)

    all_in("q1", "pm", qv)
    w_q()
    w_x()
    got("x0", lambda: xg.at[zz, oh])
    for s in range(1, n):
        got(f"cb{s}", lambda s=s: xg.at[lax.rem(zz - s + n, n), oh], zz - s >= 0)
        got(f"ca{s}", lambda s=s: xg.at[lax.rem(zz + s, n), oh], zz + s < n)
    w_tr()
    step = og.shape[0]
    for at in range(tile // step):
        rows = slice(at * step, (at + 1) * step)
        for k in range(n):
            part = xg[k, :, :, rows].reshape(2 * hr, step)
            og[:, k * LANES:(k + 1) * LANES] = lax.dot_general(
                part, cb[k].reshape(2 * hr, LANES), tn, preferred_element_type=F32).astype(BF16)
        product = jnp.dot(og[...], qg[...].reshape(n * LANES, width), preferred_element_type=F32)
        ub[rows, :] = (tr[rows, :].astype(F32) - product).astype(BF16)
        if at == 0:
            along(n - 1)
    w_up = local(4, ref(ub), ref(up_out))

    got("c0x", lambda: c0.at[:, oh], rest)
    all_in("zc", "pn", zv, rest)

    def same():
        q0g[...] = qg[...]
    on(first, same)
    blk = og0.shape[0]
    start = zz * 2 * sr
    lanes = pl.ds(pl.multiple_of(start // blk * blk, blk), blk)
    for k in range(n):
        part = xg[k, :, :, lanes].reshape(2 * hr, blk)
        og0[:, k * LANES:(k + 1) * LANES] = lax.dot_general(
            part, c0[k].reshape(2 * hr, LANES), tn, preferred_element_type=F32).astype(BF16)
    prod0[...] = jnp.dot(og0[...], q0g[...].reshape(n * LANES, width), preferred_element_type=F32)

    def finish(side, at):
        inside = pl.ds(pl.multiple_of(lax.rem(start, blk) + side * sr, sr), sr)
        nb[at] = (raw[side].astype(F32) - prod0[inside, :]).astype(BF16)

    def columns(side):
        return np_out.at[:, pl.ds(pl.multiple_of(side * width, width), width)]

    for w in w_raw:
        w()
    got("fw1", lambda: raw.at[oh], rest)
    finish(oh, 0)
    go("pfx", lambda: nb.at[0], lambda: columns(h), xn)
    got("ow1", lambda: raw.at[h], rest)
    finish(h, 1)
    w_np = local(8, lambda: nb.at[1], lambda: columns(h))
    got("pfx", lambda: columns(oh))
    for entry in pending:
        on(*entry[1:])
    w_up()
    w_np()


def hand_on(u_in, p_in, u_out, p_out, u_buf, p_buf, sems):
    parts = sems.shape[1] - 1
    size = u_in.shape[0] // parts
    views = [(p_in, p_buf, p_out)]
    for i in range(parts):
        rows = pl.ds(i * size, size)
        views.append((u_in.at[rows], u_buf.at[rows], u_out.at[rows]))
    ins = [pltpu.make_async_copy(v[0], v[1], sems.at[0, i]) for i, v in enumerate(views)]
    outs = [pltpu.make_async_copy(v[1], v[2], sems.at[1, i]) for i, v in enumerate(views)]
    for c in ins:
        c.start()
    for c, o in zip(ins, outs):
        c.wait()
        o.start()
    for o in outs:
        o.wait()


def body(trailing, left_outer, left_inner, upper_outer, upper_inner, left_ranks, upper_ranks):
    n = lax.axis_size("row")
    nc = lax.axis_size("col")
    tile, width = trailing.shape
    hr = left_outer.shape[0]
    sr = tile // nc
    blk = max(2 * sr, LANES)
    names = sem_names(n, n // 2)
    any_space = pl.BlockSpec(memory_space=pl.ANY)
    smem = pl.BlockSpec(memory_space=pltpu.SMEM)
    vmem = pltpu.VMEM
    shapes = (
        jax.ShapeDtypeStruct((tile, width), BF16),
        jax.ShapeDtypeStruct((sr, 2 * width), BF16),
    )
    results = pl.pallas_call(
        functools.partial(kernel, n, names),
        out_shape=shapes,
        in_specs=[any_space] * 5 + [smem] * 2,
        out_specs=(any_space, any_space),
        scratch_shapes=[
            vmem((n, 2, hr, tile), BF16),
            vmem((n, hr, tile), BF16),
            vmem((n, 2, LANES, width), BF16),
            vmem((n, LANES, width), BF16),
            vmem((n, LANES, width), BF16),
            vmem((n, 2, hr, LANES), BF16),
            vmem((n, 2, hr, LANES), BF16),
            vmem((512, n * LANES), BF16),
            vmem((blk, n * LANES), BF16),
            vmem((blk, width), F32),
            vmem((tile, width), BF16),
            vmem((tile, width), BF16),
            vmem((2, sr, width), BF16),
            vmem((2, sr, width), BF16),
            pltpu.SemaphoreType.DMA((len(names),)),
            pltpu.SemaphoreType.DMA((len(names),)),
            pltpu.SemaphoreType.DMA((9,)),
        ],
        compiler_params=pltpu.CompilerParams(
            collective_id=0, has_side_effects=True, vmem_limit_bytes=56 * 2 ** 20
        ),
        cost_estimate=pl.CostEstimate(
            flops=2 * tile * width * n * LANES, bytes_accessed=4 * tile * width, transcendentals=0
        ),
    )(trailing, left_outer, left_inner, upper_outer, upper_inner, left_ranks, upper_ranks)
    return pl.pallas_call(
        hand_on,
        out_shape=shapes,
        in_specs=[any_space] * 2,
        out_specs=(any_space, any_space),
        scratch_shapes=[
            vmem((tile, width), BF16),
            vmem((sr, 2 * width), BF16),
            pltpu.SemaphoreType.DMA((2, 5)),
        ],
        compiler_params=pltpu.CompilerParams(vmem_limit_bytes=56 * 2 ** 20),
    )(*results)


def solution(mesh):
    in_specs = (
        P("row", "col"),
        P("col", "row"),
        P("col", "row"),
        P("row", "col"),
        P("row", "col"),
        P(),
        P(),
    )
    out_specs = (P("row", "col"), P(("row", "col"), None))
    return jax.shard_map(body, mesh=mesh, in_specs=in_specs, out_specs=out_specs, check_vma=False)
```
